128 devices in a mesh: lat: 4 (over z), lon: 32 (over x, y, core).
Axes of the slice: x: 4, y: 4, z: 4, core: 2. Of those that a mesh axis runs over, the one named last changes fastest.
Arguments:
- latent: bfloat16 [4096, 64, 512], P(('lat', 'lon')), may hold values from -6 to 6
- patch_owner: int32 [12288, 2], P(('lat', 'lon')), may hold values from 0 to 127, all different within a row; in each aligned block of 96 rows (0 to 95, 96 to 191, ...) at most 2 rows name the same one
- patch_local: int32 [12288, 2], P(('lat', 'lon')), may hold values from 0 to 31
- obs_patch: int32 [12288, 128], P(('lat', 'lon')), may hold values from 0 to 1
- cell_offset: int32 [12288, 128], P(('lat', 'lon')), may hold values from 0 to 48
- frac: float32 [12288, 2, 128], P(('lat', 'lon')), may hold values from 0 to 1
- obs_value: float32 [12288, 128], P(('lat', 'lon')), may hold values from -6 to 6
- obs_weight: float32 [12288, 128], P(('lat', 'lon')), may hold values from 0.5 to 4
- w_hidden: bfloat16 [256, 256], replicated, may hold values from -0.375 to 0.375
- b_hidden: float32 [256], replicated, may hold values from -3 to 3
- w_out: bfloat16 [256], replicated, may hold values from -0.375 to 0.375
Outputs:
- latent_grad: float32 [4096, 64, 512], P(('lat', 'lon'))
- obs_score: float32 [12288, 128], P(('lat', 'lon'))
The draws below stay inside these ranges and needn't reach their ends.
Inputs may be any that keep to these rules, and one draw needn't show every extreme that they name: `patch_owner`: the 2 entries of a block name different devices; among the 96 blocks of one device no device is named more than 2 times, and some device exactly 2 times.
All inputs are finite; a program needn't handle non-finite values.
Results may differ from the reference program's by a relative error of at most 0.006.
Values may be sent and summed in bfloat16 or wider, within the bound.
A program may use at most 128 MiB of HBM per device.

```python
import math
import jax
import jax.numpy as jnp
import numpy as np
from jax import lax

C = 256
CELLS = 64
OB = 128
K = 2
P_DEV = 32
BLK_DEV = 96
CAP = 2
PATCHES = 4096
BLOCKS = 12288
DEVICES = 128


def place_ends(array, stream_key, least, high):
    dims = array.shape
    index_at = [jax.random.randint(jax.random.fold_in(stream_key, axis), (), 0, dims[axis]) for axis in range(len(dims))]
    array = array.at[tuple(index_at)].set(least)
    longest = dims.index(max(dims))
    index_at[longest] = (index_at[longest] + 1) % dims[longest]
    return array.at[tuple(index_at)].set(high)


def levels(rng, extent, pieces, least, largest):
    loudness = 1.0
    for position, shards_of in pieces:
        steps = jax.random.uniform(jax.random.fold_in(jax.random.fold_in(rng, 6), position), (shards_of,), jnp.float32, least / len(pieces), largest / len(pieces))
        loudness = loudness * jnp.repeat(jnp.exp(steps), extent[position] // shards_of).reshape((-1,) + (1,) * (len(extent) - 1 - position))
    return loudness


def routed_block(key, own, number, rows, amount, top, limit, lean):
    sequence = jax.random.permutation(key, amount)
    heavy_load, ordinary = load_shares(amount, rows * top, limit, lean, True), load_shares(amount, rows * top, limit, lean, False)
    places = jnp.arange(amount)

    def named(sizes, offset_by):
        used = int((sizes > 0).sum())
        fixed = max(1, used // 4)
        shifted = fixed + (places - fixed + offset_by * (used - fixed)) % max(1, amount - fixed)
        return jnp.zeros((amount,), jnp.int32).at[sequence[jnp.where(places < fixed, places, shifted)]].set(jnp.asarray(sizes, jnp.int32))

    sizes = jnp.where(number % 4 == 0, named(heavy_load, number // 4), named(ordinary, number - number // 4 - 1))
    mixed = jax.random.permutation(jax.random.fold_in(own, 3), amount)
    giver, sink = mixed[0:amount // 2 * 2:2], mixed[1:amount // 2 * 2:2]
    slack = jnp.minimum(sizes[giver] - 1, limit - sizes[sink]) // 2
    slack = jnp.where((giver == sequence[0]) | (sink == sequence[0]) | (sizes[sink] == 0), 0, jnp.maximum(slack, 0))
    shifted = jax.random.randint(jax.random.fold_in(own, 4), (amount // 2,), 0, 1 << 20) % (slack + 1)
    sizes = sizes.at[giver].add(-shifted).at[sink].add(shifted)
    members = jnp.searchsorted(jnp.cumsum(sizes), jnp.arange(rows * top), side="right").astype(jnp.int32)
    table = members.reshape(top, rows).T
    table = table[jax.random.permutation(jax.random.fold_in(own, 1), rows)]
    offset_by = jax.random.randint(jax.random.fold_in(own, 2), (rows, 1), 0, top)
    return jnp.take_along_axis(table, (jnp.arange(top)[None, :] + offset_by) % top, axis=1)


def load_shares(number_of, total, limit, lean, full):
    loads = [(1 << 20) // math.isqrt(standing ** lean) + 1 for standing in range(1, number_of + 1)]
    largest = limit if full else min(limit, max(-(-total // number_of), total * loads[0] // sum(loads)))
    least = 1 if total - largest >= number_of - 1 else 0
    given, spare = [largest] + [least] * (number_of - 1), total - largest - least * (number_of - 1)
    while spare > 0:
        free = [i for i in range(1, number_of) if given[i] < largest] or [i for i in range(1, number_of) if given[i] < limit]
        mass, remaining = sum([loads[i] for i in free]), spare
        for i in free:
            addition = min(limit - given[i], max(1, remaining * loads[i] // mass), spare)
            given[i] = given[i] + addition
            spare = spare - addition
    return np.array(given)


def noise(key, extent, deviation, limit, cuts=(), dtype=jnp.bfloat16):
    values = deviation * jax.random.normal(key, extent, jnp.float32)
    if cuts:
        values = values * levels(key, extent, cuts, -0.22, 0.18)
    return jnp.clip(values, -limit, limit).astype(dtype)


def setup_inputs(seed: int = 0) -> dict:
    seeds = jax.random.split(jax.random.key(seed), 12)
    latent = noise(seeds[0], (PATCHES, CELLS, 2 * C), 1.0, 6.0, ((0, 128),))
    patch_owner_keys = jax.random.split(jax.random.fold_in(seeds[1], 1), BLOCKS // BLK_DEV)
    patch_owner_turns = jax.random.permutation(jax.random.fold_in(seeds[1], 3), BLOCKS // BLK_DEV)
    patch_owner = jax.vmap(lambda own, number: routed_block(jax.random.fold_in(seeds[1], 2), own, number, BLK_DEV, DEVICES, K, CAP, 2))(patch_owner_keys, patch_owner_turns).reshape((BLOCKS, K))
    patch_local = place_ends(jax.random.randint(seeds[2], (BLOCKS, K), 0, P_DEV), jax.random.fold_in(seeds[2], 1), 0, P_DEV - 1).astype(jnp.int32)
    obs_patch = place_ends(jax.random.randint(seeds[3], (BLOCKS, OB), 0, K), jax.random.fold_in(seeds[3], 1), 0, K - 1).astype(jnp.int32)
    cell_offset = place_ends(jax.random.randint(seeds[4], (BLOCKS, OB), 0, 49), jax.random.fold_in(seeds[4], 1), 0, 48).astype(jnp.int32)
    frac = jnp.clip(1.0 * jax.random.uniform(seeds[5], (BLOCKS, 2, OB), jnp.float32) ** levels(seeds[5], (BLOCKS, 2, OB), ((0, 128),), -0.2, 0.2), 0.0, 1.0)
    obs_value = noise(seeds[6], (BLOCKS, OB), 1.0, 6.0, ((0, 128),), jnp.float32)
    obs_weight = jnp.clip(jnp.exp(math.log(4.0) - 2.0794415 * jax.random.uniform(seeds[7], (BLOCKS, OB), jnp.float32) ** levels(seeds[7], (BLOCKS, OB), ((0, 128),), -0.2, 0.2)), 0.5, 4.0)
    w_hidden = noise(seeds[8], (C, C), C ** -0.5, 0.375)
    b_hidden = noise(seeds[9], (C,), 0.5, 3.0, (), jnp.float32)
    w_out = noise(seeds[10], (C,), C ** -0.5, 0.375)
    return {"latent": latent, "patch_owner": patch_owner, "patch_local": patch_local, "obs_patch": obs_patch, "cell_offset": cell_offset, "frac": frac, "obs_value": obs_value, "obs_weight": obs_weight, "w_hidden": w_hidden, "b_hidden": b_hidden, "w_out": w_out}


root_coef = 0.7978845608028654
cubic_coef = 0.044715
smooth_sq = 0.01
loss_scale = 64.0

def gelu_pair(pre_act):
    inner_arg = root_coef * (pre_act + cubic_coef * pre_act * pre_act * pre_act)
    tangent = jnp.tanh(inner_arg)
    result = 0.5 * pre_act * (1.0 + tangent)
    derivative = 0.5 * (1.0 + tangent) + 0.5 * pre_act * (1.0 - tangent * tangent) * root_coef * (1.0 + 3.0 * cubic_coef * pre_act * pre_act)
    return (result, derivative)

def decode(sampled, w_hidden, b_hidden, w_out, obs_vals, obs_wts):
    n_rows = sampled.shape[0]
    n_chan = w_hidden.shape[0]
    inputs = sampled.reshape(n_rows * 2, n_chan)
    pre_act = jnp.dot(inputs, w_hidden, preferred_element_type=jnp.float32) + b_hidden
    activ, derivative = gelu_pair(pre_act)
    activ = activ.astype(jnp.bfloat16)
    predicted = jnp.dot(activ, w_out, preferred_element_type=jnp.float32).reshape(n_rows, 2)
    member_one = predicted[:, 0]
    member_two = predicted[:, 1]
    err_one = member_one - obs_vals
    err_two = member_two - obs_vals
    between = member_one - member_two
    soft_one = jnp.sqrt(err_one * err_one + smooth_sq)
    soft_two = jnp.sqrt(err_two * err_two + smooth_sq)
    soft_mid = jnp.sqrt(between * between + smooth_sq)
    penalty = obs_wts * (0.5 * (soft_one + soft_two) - 0.5 * soft_mid)
    scaled = 0.5 * loss_scale * obs_wts
    grad_one = scaled * (err_one / soft_one - between / soft_mid)
    grad_two = scaled * (err_two / soft_two + between / soft_mid)
    grad_pred = jnp.stack([grad_one, grad_two], axis=1).reshape(n_rows * 2)
    delta = (grad_pred[:, None] * w_out.astype(jnp.float32)[None, :] * derivative).astype(jnp.bfloat16)
    back_grad = jnp.dot(delta, w_hidden.T, preferred_element_type=jnp.float32).reshape(n_rows, 2 * n_chan)
    return (penalty, back_grad.astype(jnp.bfloat16))

def pick_rows(patch_rows, index):
    return patch_rows[index]

def add_rows(grad_rows, index, update):
    return grad_rows.at[index].add(update)

def rounded_weight(value):
    return lax.optimization_barrier(value.astype(jnp.bfloat16)).astype(jnp.float32)

def reference(latent, patch_owner, patch_local, obs_patch, cell_offset, frac, obs_value, obs_weight, w_hidden, b_hidden, w_out):
    n_cols = latent.shape[2]
    global_ids = (patch_owner * P_DEV + patch_local).astype(jnp.int32)
    per_step = math.gcd(BLOCKS, 64)
    n_steps = BLOCKS // per_step

    def one_step(carry, inputs):
        ids_g, entry_g, offset_g, frac_g, value_g, weight_g = inputs
        patch_rows = jnp.take(latent, ids_g.reshape(per_step * K), axis=0)
        patch_rows = patch_rows.reshape(per_step, K * CELLS, n_cols).astype(jnp.float32)
        row_part = offset_g // 7
        col_part = offset_g % 7
        corner = (entry_g * CELLS + row_part * 8 + col_part).astype(jnp.int32)
        frac_lat = frac_g[:, 0, :]
        frac_lon = frac_g[:, 1, :]
        coefs = [(1.0 - frac_lat) * (1.0 - frac_lon), (1.0 - frac_lat) * frac_lon, frac_lat * (1.0 - frac_lon), frac_lat * frac_lon]
        coefs = [rounded_weight(coef) for coef in coefs]
        shifts = [0, 1, 8, 9]
        sampled = jnp.zeros((per_step, OB, n_cols), jnp.float32)
        for shift, coef in zip(shifts, coefs):
            picked = jax.vmap(pick_rows)(patch_rows, corner + shift)
            sampled = sampled + coef[:, :, None] * picked
        sampled = sampled.astype(jnp.bfloat16)
        penalty, back_grad = decode(sampled.reshape(per_step * OB, n_cols), w_hidden, b_hidden, w_out, value_g.reshape(per_step * OB), weight_g.reshape(per_step * OB))
        back_grad = back_grad.astype(jnp.float32).reshape(per_step, OB, n_cols)
        grad_rows = jnp.zeros((per_step, K * CELLS, n_cols), jnp.float32)
        for shift, coef in zip(shifts, coefs):
            grad_rows = jax.vmap(add_rows)(grad_rows, corner + shift, coef[:, :, None] * back_grad)
        rounded = lax.optimization_barrier(grad_rows.astype(jnp.bfloat16))
        rounded = rounded.astype(jnp.float32).reshape(per_step * K, CELLS, n_cols)
        carry = carry.at[ids_g.reshape(per_step * K)].add(rounded)
        return (carry, penalty.reshape(per_step, OB))
    packed = (global_ids.reshape(n_steps, per_step, K), obs_patch.reshape(n_steps, per_step, OB), cell_offset.reshape(n_steps, per_step, OB), frac.reshape(n_steps, per_step, 2, OB), obs_value.reshape(n_steps, per_step, OB), obs_weight.reshape(n_steps, per_step, OB))
    init = jnp.zeros((PATCHES, CELLS, n_cols), jnp.float32)
    latent_grad, scores = lax.scan(one_step, init, packed)
    return (latent_grad, scores.reshape(BLOCKS, OB))
```

```python
import jax
import jax.numpy as jnp
from jax import lax
from jax.experimental import pallas as pl
from jax.experimental.pallas import tpu as pltpu
from jax.sharding import PartitionSpec as P

root_coef = 0.7978845608028654
cubic_coef = 0.044715
smooth_sq = 0.01
loss_scale = 64.0

alpha = (1.0 / (root_coef * cubic_coef)) ** (1.0 / 3.0)
beta = root_coef * alpha

AXES = ("lat", "lon")
F32, BF16 = jnp.float32, jnp.bfloat16
VMEM = pl.BlockSpec(memory_space=pltpu.VMEM)
SMEM = pl.BlockSpec(memory_space=pltpu.SMEM)


def three_parts(x):
    high = x.astype(BF16)
    rest = x - high.astype(F32)
    mid = rest.astype(BF16)
    return (high, mid, (rest - mid.astype(F32)).astype(BF16))


def pick(sel, x, dims):
    return sum(
        lax.dot_general(sel, part, (dims, ((), ())), preferred_element_type=F32)
        for part in three_parts(x)
    )


def selectors(owner):
    n = owner.shape[0]
    devices = lax.broadcasted_iota(jnp.int32, (n, 128), 1)
    hit = [(owner[:, e : e + 1] == devices) for e in range(2)]
    both = jnp.where(hit[0] | hit[1], 1.0, 0.0).astype(BF16)
    before = lax.broadcasted_iota(jnp.int32, (n, n), 0) > lax.broadcasted_iota(
        jnp.int32, (n, n), 1
    )
    before = jnp.where(before, 1.0, 0.0).astype(BF16)
    rank = jnp.dot(before, both, preferred_element_type=F32)
    return [
        [jnp.where(hit[e] & (rank == k), 1.0, 0.0) for e in range(2)] for k in range(2)
    ]


def pack_kernel(owner, local, entry, offset, frac, value, weight, out, ids):
    sel = selectors(owner[...])
    off = offset[...]
    row = lax.shift_right_logical(off * 37, 8)
    col = off - row * 7
    pos_lat = frac[:, 0, :] + row.astype(F32)
    pos_lon = frac[:, 1, :] + col.astype(F32)
    data = jnp.concatenate([pos_lat, pos_lon, value[...]], axis=1)
    wts = weight[...]
    where = entry[...]
    wts = jnp.concatenate(
        [jnp.where(where == 0, wts, 0.0), jnp.where(where == 1, wts, 0.0)], axis=0
    )
    loc = local[...].astype(F32) + 1.0
    name = []
    for k in range(2):
        one = (sel[k][0] + sel[k][1]).astype(BF16)
        got = pick(one, data, ((0,), (0,)))
        for f in range(3):
            out[:, k, f, :] = got[:, f * 128 : (f + 1) * 128]
        two = jnp.concatenate(sel[k], axis=0).astype(BF16)
        out[:, k, 3, :] = pick(two, wts, ((0,), (0,)))
        both = jnp.concatenate(
            [jnp.broadcast_to(loc[:, e : e + 1], sel[k][e].shape) for e in range(2)], axis=0
        ).astype(BF16)
        name.append(
            lax.dot_general(two, both, (((0,), (0,)), ((), ())), preferred_element_type=F32)
        )
    lane = lax.broadcasted_iota(jnp.int32, name[0].shape, 1)
    ids[...] = jnp.where(lane == 0, name[0], name[1]).astype(jnp.int32)[:, :2] - 1


def compute_kernel(
    ids,
    latent,
    recv,
    w_hidden,
    b_hidden,
    w_out,
    grad,
    score,
    left,
    deriv,
    total,
    w_t,
    bias,
    head,
    pend,
    pair_p,
    pair_a,
    pair_b,
):
    n_patch = latent.shape[0]
    n_slot = recv.shape[0]
    lane = lax.broadcasted_iota(jnp.int32, (256, 128), 1)

    for p in range(n_patch + 1):
        pend[p] = -1

    def add_slot(s, n):
        p = ids[s]
        at = jnp.where(p < 0, n_patch, p)
        prev = pend[at]
        pair_p[n] = at
        pair_a[n] = prev
        pair_b[n] = s
        full = prev >= 0
        pend[at] = jnp.where(full | (p < 0), -1, s)
        return n + jnp.where(full, 1, 0)

    n_pair = lax.fori_loop(0, n_slot, add_slot, 0)

    def add_rest(p, n):
        prev = pend[p]
        pair_p[n] = p
        pair_a[n] = prev
        pair_b[n] = -1
        return n + jnp.where(prev >= 0, 1, 0)

    n_pair = lax.fori_loop(0, n_patch, add_rest, n_pair)

    w_t[...] = w_hidden[...].astype(F32).T.astype(BF16)
    b_parts = three_parts(jnp.broadcast_to(b_hidden[...] * (1.0 / alpha), (128, 256)).T)
    bias[...] = jnp.where(
        lane == 0,
        b_parts[0],
        jnp.where(lane == 1, b_parts[1], jnp.where(lane == 2, b_parts[2], jnp.zeros_like(b_parts[0]))),
    )
    head[...] = jnp.broadcast_to(w_out[...].astype(F32), (128, 256)).T

    def project(p, c):
        rows = latent[p]
        for m in range(2):
            twice = jnp.concatenate([rows[:, m * 256 : (m + 1) * 256]] * 2, axis=0)
            full = lax.dot_general(
                w_t[...], twice, (((1,), (1,)), ((), ())), preferred_element_type=F32
            ) * (1.0 / alpha)
            high = full.astype(BF16)
            low = (full - high.astype(F32)).astype(BF16)
            left[p, m * 256 : (m + 1) * 256, :] = jnp.where(lane < 64, high, low)
        total[p] = jnp.zeros(total.shape[1:], F32)
        return c

    lax.fori_loop(0, n_patch, project, 0)
    score[...] = jnp.zeros(score.shape, F32)

    cells = lax.broadcasted_iota(jnp.int32, (8, 256), 0).astype(F32)
    ones = jnp.ones((128, 256), BF16)

    def one_pair(i, c):
        p, a, b = pair_p[i], pair_a[i], pair_b[i]
        first, second = recv[a], recv[jnp.maximum(b, 0)]
        obs = jnp.concatenate([first, second], axis=1)
        lat = jnp.maximum(1.0 - jnp.abs(obs[0:1] - cells), 0.0)
        lon = jnp.maximum(1.0 - jnp.abs(obs[1:2] - cells), 0.0)
        corner = jnp.concatenate([lat[r : r + 1] * lon for r in range(8)], axis=0)
        corner_b = corner.astype(BF16)
        right = jnp.concatenate([corner_b, corner_b, ones], axis=0)
        pred = []
        for m in range(2):
            acc = jnp.zeros((8, 256), F32)
            for q in range(4):
                at = m * 256 + q * 64
                lhs = jnp.concatenate(
                    [left[p, at : at + 64, :], bias[q * 64 : q * 64 + 64, :]], axis=1
                )
                v = jnp.dot(lhs, right, preferred_element_type=F32)
                v2 = v * v
                u = jnp.tanh(v * (v2 + beta))
                h = 1.0 + u
                deriv[at : at + 64, :] = (
                    h * (1.0 / 3.0 + (1.0 - u) * (v * (v2 + beta / 3.0)))
                ).astype(BF16)
                wo = head[q * 64 : q * 64 + 64, :]
                act = v * h * jnp.concatenate([wo, wo], axis=1)
                acc = acc + jnp.sum(act.reshape(8, 8, 256), axis=0)
            pred.append(jnp.sum(acc, axis=0, keepdims=True) * (0.5 * alpha))
        value = obs[2:3]
        wts = obs[3:4]
        keep = jnp.where(b >= 0, 1.0, 0.0)
        wts = jnp.concatenate([wts[:, :128], wts[:, 128:] * keep], axis=1)
        e0, e1, between = pred[0] - value, pred[1] - value, pred[0] - pred[1]
        s0, s1, sm = (x * x + smooth_sq for x in (e0, e1, between))
        r0, r1, rm = (lax.rsqrt(x) for x in (s0, s1, sm))
        pen = wts * (0.5 * (s0 * r0 + s1 * r1) - 0.5 * (sm * rm))
        score[pl.ds(a, 1), :] = pen[:, :128]
        score[pl.ds(jnp.where(b < 0, n_slot, b), 1), :] = pen[:, 128:]
        mid = between * rm
        scaled = (0.5 * loss_scale) * wts
        back = jnp.concatenate(
            [corner * (scaled * (e0 * r0 - mid)), corner * (scaled * (e1 * r1 + mid))], axis=0
        ).astype(BF16)
        total[p] += lax.dot_general(
            deriv[...], back, (((1,), (1,)), ((), ())), preferred_element_type=F32
        )
        return c

    lax.fori_loop(0, n_pair, one_pair, 0)

    def finish(p, c):
        both = jnp.where(lane < 64, total[p, 0:256, :], total[p, 256:512, :])
        both = both * (1.5 * head[...])
        high = both.astype(BF16)
        low = (both - high.astype(F32)).astype(BF16)
        dims = (((0,), (0,)), ((), ()))
        res = lax.dot_general(high, w_t[...], dims, preferred_element_type=F32)
        res = res + lax.dot_general(low, w_t[...], dims, preferred_element_type=F32)
        grad[p, :, 0:256] = res[0:64]
        grad[p, :, 256:512] = res[64:128]
        return c

    lax.fori_loop(0, n_patch, finish, 0)


def unpack_kernel(owner, entry, back, out):
    sel = selectors(owner[...])
    got = []
    for e in range(2):
        got.append(
            sum(pick(sel[k][e].astype(BF16), back[:, k, :], ((1,), (0,))) for k in range(2))
        )
    out[...] = jnp.where(entry[...] == 0, got[0], got[1])


def per_device(
    latent,
    patch_owner,
    patch_local,
    obs_patch,
    cell_offset,
    frac,
    obs_value,
    obs_weight,
    w_hidden,
    b_hidden,
    w_out,
):
    n_patch = latent.shape[0]
    limit = pltpu.CompilerParams(vmem_limit_bytes=60 * 1024 * 1024)
    sent, names = pl.pallas_call(
        pack_kernel,
        out_shape=(
            jax.ShapeDtypeStruct((128, 2, 4, 128), F32),
            jax.ShapeDtypeStruct((128, 2), jnp.int32),
        ),
        in_specs=[VMEM] * 7,
        out_specs=(VMEM, VMEM),
        compiler_params=limit,
    )(patch_owner, patch_local, obs_patch, cell_offset, frac, obs_value, obs_weight)
    recv = lax.all_to_all(sent.reshape(256, 4, 128), AXES, 0, 0, tiled=True)
    ids = lax.all_to_all(names, AXES, 0, 0, tiled=True)
    grad, score = pl.pallas_call(
        compute_kernel,
        out_shape=(
            jax.ShapeDtypeStruct(latent.shape, F32),
            jax.ShapeDtypeStruct((264, 128), F32),
        ),
        in_specs=[SMEM] + [VMEM] * 5,
        out_specs=(VMEM, VMEM),
        scratch_shapes=[
            pltpu.VMEM((n_patch, 512, 128), BF16),
            pltpu.VMEM((512, 256), BF16),
            pltpu.VMEM((n_patch, 512, 128), F32),
            pltpu.VMEM((256, 256), BF16),
            pltpu.VMEM((256, 128), BF16),
            pltpu.VMEM((256, 128), F32),
            pltpu.SMEM((n_patch + 1,), jnp.int32),
            pltpu.SMEM((296,), jnp.int32),
            pltpu.SMEM((296,), jnp.int32),
            pltpu.SMEM((296,), jnp.int32),
        ],
        compiler_params=limit,
    )(
        ids.reshape(256),
        latent,
        recv,
        w_hidden,
        b_hidden.reshape(1, 256),
        w_out.reshape(1, 256),
    )
    back = lax.all_to_all(score[:256].reshape(128, 2, 128), AXES, 0, 0, tiled=True)
    obs_score = pl.pallas_call(
        unpack_kernel,
        out_shape=jax.ShapeDtypeStruct(obs_value.shape, F32),
        in_specs=[VMEM] * 3,
        out_specs=VMEM,
        compiler_params=limit,
    )(patch_owner, obs_patch, back)
    return (grad, obs_score)


def solution(mesh):
    rows2 = P(AXES, None)
    rows3 = P(AXES, None, None)
    return jax.shard_map(
        per_device,
        mesh=mesh,
        in_specs=(rows3, rows2, rows2, rows2, rows2, rows3, rows2, rows2, P(), P(), P()),
        out_specs=(rows3, rows2),
        check_vma=False,
    )
```

```python
import jax
import jax.numpy as jnp
from jax import lax
from jax.experimental import pallas as pl
from jax.experimental.pallas import tpu as pltpu
from jax.sharding import PartitionSpec as P

root_coef = 0.7978845608028654
cubic_coef = 0.044715
smooth_sq = 0.01
loss_scale = 64.0

alpha = (1.0 / (root_coef * cubic_coef)) ** (1.0 / 3.0)
beta = root_coef * alpha

AXES = ("lat", "lon")
F32, BF16 = jnp.float32, jnp.bfloat16
VMEM = pl.BlockSpec(memory_space=pltpu.VMEM)
SMEM = pl.BlockSpec(memory_space=pltpu.SMEM)
UNROLL = 4
TILES = 168


def three_parts(x):
    high = x.astype(BF16)
    rest = x - high.astype(F32)
    mid = rest.astype(BF16)
    return (high, mid, (rest - mid.astype(F32)).astype(BF16))


def pick(sel, x, dims):
    return sum(
        lax.dot_general(sel, part, (dims, ((), ())), preferred_element_type=F32)
        for part in three_parts(x)
    )


def selectors(owner):
    n = owner.shape[0]
    devices = lax.broadcasted_iota(jnp.int32, (n, 128), 1)
    hit = [(owner[:, e : e + 1] == devices) for e in range(2)]
    both = jnp.where(hit[0] | hit[1], 1.0, 0.0).astype(BF16)
    before = lax.broadcasted_iota(jnp.int32, (n, n), 0) > lax.broadcasted_iota(
        jnp.int32, (n, n), 1
    )
    before = jnp.where(before, 1.0, 0.0).astype(BF16)
    rank = jnp.dot(before, both, preferred_element_type=F32)
    return [
        [jnp.where(hit[e] & (rank == k), 1.0, 0.0) for e in range(2)] for k in range(2)
    ]


def ones_before(entry):
    first = lax.broadcasted_iota(jnp.int32, (128, 128), 0)
    second = lax.broadcasted_iota(jnp.int32, (128, 128), 1)
    tri = jnp.where(first < second, 1.0, 0.0).astype(BF16)
    mine = jnp.where(entry == 1, 1.0, 0.0).astype(BF16)
    return jnp.dot(mine, tri, preferred_element_type=F32).astype(jnp.int32)


def pack(owner, local, entry, offset, frac, value, weight, out):
    sel = selectors(owner[...])
    off = offset[...]
    row = lax.shift_right_logical(off * 37, 8)
    col = off - row * 7
    fields = [frac[:, 0, :] + row.astype(F32), frac[:, 1, :] + col.astype(F32)]
    fields += [value[...], weight[...]]
    where = entry[...]
    lane = lax.broadcasted_iota(jnp.int32, where.shape, 1)
    one = ones_before(where)
    loc = local[...].astype(F32) + 1.0
    data, names = [], []
    for e in range(2):
        gap = one if e == 0 else lane - one
        word = jnp.where(where == e, (1 << 20) + gap * 256 + lane, 0)
        for k in range(7):
            come = pltpu.roll(word, 128 - (1 << k), 1)
            stay = jnp.where((word & (256 << k)) == 0, word, 0)
            word = jnp.where((come & (256 << k)) != 0, come, stay)
        source = word & 127
        used = word >= (1 << 20)
        moved = [jnp.take_along_axis(x, source, axis=1) for x in fields]
        moved[3] = jnp.where(used, moved[3], 0.0)
        data.append(jnp.concatenate(moved, axis=1))
        count = jnp.sum(jnp.where(used, 1.0, 0.0), axis=1, keepdims=True)
        names.append(jnp.where(lane < 2, loc[:, e : e + 1], count))
    data = jnp.concatenate(data, axis=0)
    names = jnp.concatenate(names, axis=0).astype(BF16)
    got = []
    for k in range(2):
        two = jnp.concatenate(sel[k], axis=0).astype(BF16)
        rows = pick(two, data, ((0,), (0,)))
        for f in range(4):
            out[:, 4 * k + f, :] = rows[:, f * 128 : (f + 1) * 128]
        got.append(
            lax.dot_general(two, names, (((0,), (0,)), ((), ())), preferred_element_type=F32)
        )
    lane = lax.broadcasted_iota(jnp.int32, (128, 128), 1)
    out[:, 8, :] = jnp.where((lane & 1) == 0, got[0], got[1])


def send_kernel(
    owner,
    local,
    entry,
    offset,
    frac,
    value,
    weight,
    latent,
    w_hidden,
    recv,
    meta,
    left,
    sent,
    w_t,
    send_sem,
    recv_sem,
):
    lat_size, lon_size = lax.axis_size("lat"), lax.axis_size("lon")
    n_dev = lat_size * lon_size
    me = lax.axis_index("lat") * lon_size + lax.axis_index("lon")
    mesh_id = pl.DeviceIdType.MESH

    def place(i):
        j = lax.rem(me + i, n_dev)
        return j, (lax.div(j, lon_size), lax.rem(j, lon_size))

    barrier = pltpu.get_barrier_semaphore()

    def greet(i, c):
        pl.semaphore_signal(barrier, inc=1, device_id=place(i)[1], device_id_type=mesh_id)
        return c

    lax.fori_loop(1, n_dev, greet, 0)
    pack(owner, local, entry, offset, frac, value, weight, sent)
    pl.semaphore_wait(barrier, n_dev - 1)

    def send(i, c):
        j, there = place(i)
        pltpu.make_async_remote_copy(
            src_ref=sent.at[j],
            dst_ref=recv.at[me],
            send_sem=send_sem,
            recv_sem=recv_sem,
            device_id=there,
            device_id_type=mesh_id,
        ).start()
        return c

    lax.fori_loop(1, n_dev, send, 0)
    recv[me] = sent[me]

    w_t[...] = w_hidden[...].astype(F32).T.astype(BF16)
    lane = lax.broadcasted_iota(jnp.int32, (256, 128), 1)

    def project(p, c):
        rows = latent[p]
        for m in range(2):
            twice = jnp.concatenate([rows[:, m * 256 : (m + 1) * 256]] * 2, axis=0)
            full = lax.dot_general(
                w_t[...], twice, (((1,), (1,)), ((), ())), preferred_element_type=F32
            ) * (1.0 / alpha)
            high = full.astype(BF16)
            low = (full - high.astype(F32)).astype(BF16)
            left[p, m * 256 : (m + 1) * 256, :] = jnp.where(lane < 64, high, low)
        return c

    lax.fori_loop(0, latent.shape[0], project, 0)
    pltpu.make_async_remote_copy(
        src_ref=sent.at[pl.ds(0, n_dev - 1)],
        dst_ref=recv.at[pl.ds(0, n_dev - 1)],
        send_sem=send_sem,
        recv_sem=recv_sem,
        device_id=place(1)[1],
        device_id_type=mesh_id,
    ).wait()
    meta[...] = recv[:, 8, :].T[0:8].astype(jnp.int32)


def compute_kernel(
    meta,
    left,
    recv,
    w_hidden,
    b_hidden,
    w_out,
    grad,
    score,
    total,
    w_t,
    bias,
    head,
    comp,
    dense,
    fill,
    tile_p,
    slot_at,
    slot_next,
    *bufs,
):
    n_patch = left.shape[0]
    n_dev = recv.shape[0]
    derivs, pres = bufs[:UNROLL], bufs[UNROLL:]
    lane = lax.broadcasted_iota(jnp.int32, (256, 128), 1)
    lane4 = lax.broadcasted_iota(jnp.int32, (4, 128), 1)
    lane1 = lax.broadcasted_iota(jnp.int32, (1, 128), 1)

    for p in range(n_patch + 1):
        fill[p] = 0
    comp[...] = jnp.zeros(comp.shape, F32)
    dense[...] = jnp.zeros(dense.shape, F32)

    def append(s, n_tile):
        rows = recv[s]
        for k in range(2):
            name, n = meta[k, s], meta[2 + k, s]
            p = jnp.where(name == 0, n_patch, name - 1)
            at = fill[p]
            closed = (at & 255) == 0
            base = jnp.where(closed, n_tile * 256, at)
            tile_p[jnp.where(closed, n_tile, TILES - 1)] = jnp.minimum(p, n_patch - 1)
            n_tile = n_tile + jnp.where(closed & (n > 0), 1, 0)
            half, shift = lax.shift_right_logical(base, 7), base & 127
            odd = half & 1
            over = (odd == 1) & (shift + n > 128)
            after = jnp.where(odd == 1, n_tile * 2, half + 1)
            tile_p[jnp.where(over, n_tile, TILES - 1)] = p
            fill[p] = jnp.where(
                n == 0, at, jnp.where(over, n_tile * 256 + shift + n - 128, base + n)
            )
            n_tile = n_tile + jnp.where(over, 1, 0)
            slot_at[2 * s + k] = base
            slot_next[2 * s + k] = after
            turned = pltpu.roll(rows[4 * k : 4 * k + 4], shift, 1)
            comp[half] = jnp.where(lane4 >= shift, turned, comp[half])
            comp[after] = jnp.where(lane4 < shift, turned, 0.0)
        return n_tile

    n_tile = lax.fori_loop(0, n_dev, append, 0)
    for j in range(UNROLL):
        tile_p[n_tile + j] = 0

    w_t[...] = w_hidden[...].astype(F32).T.astype(BF16)
    b_parts = three_parts(jnp.broadcast_to(b_hidden[...] * (1.0 / alpha), (128, 256)).T)
    column = jnp.where(
        lane == 0,
        b_parts[0],
        jnp.where(
            lane == 1, b_parts[1], jnp.where(lane == 2, b_parts[2], jnp.zeros_like(b_parts[0]))
        ),
    )
    bias[0:256, :] = column
    bias[256:512, :] = column
    head[...] = jnp.broadcast_to(w_out[...].astype(F32), (128, 256)).T

    def clear(p, c):
        total[p] = jnp.zeros(total.shape[1:], F32)
        return c

    lax.fori_loop(0, n_patch, clear, 0)

    cells = lax.broadcasted_iota(jnp.int32, (8, 256), 0).astype(F32)
    ones = jnp.ones((128, 256), BF16)

    def forward(i, deriv, pre):
        obs = jnp.concatenate([comp[2 * i], comp[2 * i + 1]], axis=1)
        lat = jnp.maximum(1.0 - jnp.abs(obs[0:1] - cells), 0.0)
        lon = jnp.maximum(1.0 - jnp.abs(obs[1:2] - cells), 0.0)
        corner = jnp.concatenate([lat[r : r + 1] * lon for r in range(8)], axis=0)
        corner_b = corner.astype(BF16)
        right = jnp.concatenate([corner_b, corner_b, ones], axis=0)
        lhs = jnp.concatenate([left[tile_p[i]], bias[...]], axis=1)
        pre[...] = jnp.dot(lhs, right, preferred_element_type=F32)
        pred = []
        for m in range(2):
            acc = jnp.zeros((8, 256), F32)
            for q in range(4):
                at = m * 256 + q * 64
                v = pre[at : at + 64, :]
                v2 = v * v
                u = jnp.tanh(v * (v2 + beta))
                h = 1.0 + u
                v_b, w_b, h_b = v.astype(BF16), (1.0 - u).astype(BF16), h.astype(BF16)
                slope = v_b * (v_b * v_b + BF16(beta / 3.0))
                deriv[at : at + 64, :] = h_b * (BF16(1.0 / 3.0) + w_b * slope)
                wo = head[q * 64 : q * 64 + 64, :]
                act = v * h * jnp.concatenate([wo, wo], axis=1)
                acc = acc + jnp.sum(act.reshape(8, 8, 256), axis=0)
            pred.append(jnp.sum(acc, axis=0, keepdims=True) * (0.5 * alpha))
        return obs, corner, pred

    def loss(i, obs, pred):
        value = obs[2:3]
        wts = obs[3:4]
        e0, e1, between = pred[0] - value, pred[1] - value, pred[0] - pred[1]
        s0, s1, sm = (x * x + smooth_sq for x in (e0, e1, between))
        r0, r1, rm = (lax.rsqrt(x) for x in (s0, s1, sm))
        pen = wts * (0.5 * (s0 * r0 + s1 * r1) - 0.5 * (sm * rm))
        dense[pl.ds(2 * i, 1), :] = pen[:, :128]
        dense[pl.ds(2 * i + 1, 1), :] = pen[:, 128:]
        mid = between * rm
        scaled = (0.5 * loss_scale) * wts
        return scaled * (e0 * r0 - mid), scaled * (e1 * r1 + mid)

    def backward(i, corner, g, deriv):
        back = jnp.concatenate([corner * g[0], corner * g[1]], axis=0).astype(BF16)
        total[tile_p[i]] += lax.dot_general(
            deriv[...], back, (((1,), (1,)), ((), ())), preferred_element_type=F32
        )

    def some_tiles(i, c):
        base = i * UNROLL
        fw = [forward(base + j, derivs[j], pres[j]) for j in range(UNROLL)]
        gs = [loss(base + j, fw[j][0], fw[j][2]) for j in range(UNROLL)]
        for j in range(UNROLL):
            backward(base + j, fw[j][1], gs[j], derivs[j])
        return c

    lax.fori_loop(0, lax.div(n_tile + UNROLL - 1, UNROLL), some_tiles, 0)

    def give(i, c):
        for j in range(8):
            s = 8 * i + j
            base = slot_at[s]
            half, shift = lax.shift_right_logical(base, 7), base & 127
            row = jnp.where(
                lane1 >= shift, dense[pl.ds(half, 1), :], dense[pl.ds(slot_next[s], 1), :]
            )
            score[pl.ds(s, 1), :] = pltpu.roll(row, (128 - shift) & 127, 1)
        return c

    lax.fori_loop(0, n_dev // 4, give, 0)

    def finish(i, c):
        for j in range(2):
            p = 2 * i + j
            both = jnp.where(lane < 64, total[p, 0:256, :], total[p, 256:512, :])
            both = both * (1.5 * head[...])
            high = both.astype(BF16)
            low = (both - high.astype(F32)).astype(BF16)
            dims = (((0,), (0,)), ((), ()))
            res = lax.dot_general(high, w_t[...], dims, preferred_element_type=F32)
            res = res + lax.dot_general(low, w_t[...], dims, preferred_element_type=F32)
            grad[p, :, 0:256] = res[0:64]
            grad[p, :, 256:512] = res[64:128]
        return c

    lax.fori_loop(0, n_patch // 2, finish, 0)


def unpack_kernel(owner, entry, back, out):
    sel = selectors(owner[...])
    where = entry[...]
    lane = lax.broadcasted_iota(jnp.int32, where.shape, 1)
    one = ones_before(where)
    got = []
    for e in range(2):
        rows = sum(pick(sel[k][e].astype(BF16), back[:, k, :], ((1,), (0,))) for k in range(2))
        got.append(jnp.take_along_axis(rows, one if e == 1 else lane - one, axis=1))
    out[...] = jnp.where(where == 0, got[0], got[1])


def send(patch_owner, patch_local, obs_patch, cell_offset, frac, obs_value, obs_weight, latent, w_hidden):
    n_patch = latent.shape[0]
    return pl.pallas_call(
        send_kernel,
        out_shape=(
            jax.ShapeDtypeStruct((128, 9, 128), F32),
            jax.ShapeDtypeStruct((8, 128), jnp.int32),
            jax.ShapeDtypeStruct((n_patch, 512, 128), BF16),
        ),
        in_specs=[VMEM] * 9,
        out_specs=(VMEM, VMEM, VMEM),
        scratch_shapes=[
            pltpu.VMEM((128, 9, 128), F32),
            pltpu.VMEM((256, 256), BF16),
            pltpu.SemaphoreType.DMA,
            pltpu.SemaphoreType.DMA,
        ],
        compiler_params=pltpu.CompilerParams(
            vmem_limit_bytes=60 * 1024 * 1024, collective_id=0, has_side_effects=True
        ),
    )(patch_owner, patch_local, obs_patch, cell_offset, frac, obs_value, obs_weight, latent, w_hidden)


def compute(meta, left, recv, w_hidden, b_hidden, w_out):
    n_patch = left.shape[0]
    return pl.pallas_call(
        compute_kernel,
        out_shape=(
            jax.ShapeDtypeStruct((n_patch, 64, 512), F32),
            jax.ShapeDtypeStruct((256, 128), F32),
        ),
        in_specs=[SMEM] + [VMEM] * 5,
        out_specs=(VMEM, VMEM),
        scratch_shapes=[
            pltpu.VMEM((n_patch, 512, 128), F32),
            pltpu.VMEM((256, 256), BF16),
            pltpu.VMEM((512, 128), BF16),
            pltpu.VMEM((256, 128), F32),
            pltpu.VMEM((2 * TILES, 4, 128), F32),
            pltpu.VMEM((2 * TILES, 128), F32),
            pltpu.SMEM((n_patch + 1,), jnp.int32),
            pltpu.SMEM((TILES,), jnp.int32),
            pltpu.SMEM((256,), jnp.int32),
            pltpu.SMEM((256,), jnp.int32),
        ]
        + [pltpu.VMEM((512, 256), BF16)] * UNROLL
        + [pltpu.VMEM((512, 256), F32)] * UNROLL,
        compiler_params=pltpu.CompilerParams(vmem_limit_bytes=60 * 1024 * 1024),
    )(meta, left, recv, w_hidden, b_hidden.reshape(1, 256), w_out.reshape(1, 256))


def unpack(patch_owner, obs_patch, back):
    return pl.pallas_call(
        unpack_kernel,
        out_shape=jax.ShapeDtypeStruct(obs_patch.shape, F32),
        in_specs=[VMEM] * 3,
        out_specs=VMEM,
        compiler_params=pltpu.CompilerParams(vmem_limit_bytes=60 * 1024 * 1024),
    )(patch_owner, obs_patch, back)


def per_device(
    latent,
    patch_owner,
    patch_local,
    obs_patch,
    cell_offset,
    frac,
    obs_value,
    obs_weight,
    w_hidden,
    b_hidden,
    w_out,
):
    recv, meta, left = send(
        patch_owner, patch_local, obs_patch, cell_offset, frac, obs_value, obs_weight, latent, w_hidden
    )
    grad, score = compute(meta, left, recv, w_hidden, b_hidden, w_out)
    back = lax.all_to_all(score.reshape(128, 2, 128), AXES, 0, 0, tiled=True)
    return (grad, unpack(patch_owner, obs_patch, back))


def solution(mesh):
    rows2 = P(AXES, None)
    rows3 = P(AXES, None, None)
    return jax.shard_map(
        per_device,
        mesh=mesh,
        in_specs=(rows3, rows2, rows2, rows2, rows2, rows3, rows2, rows2, P(), P(), P()),
        out_specs=(rows3, rows2),
        check_vma=False,
    )
```

```python
import jax
import jax.numpy as jnp
from jax import lax
from jax.experimental import pallas as pl
from jax.experimental.pallas import tpu as pltpu
from jax.sharding import PartitionSpec as P

root_coef = 0.7978845608028654
cubic_coef = 0.044715
smooth_sq = 0.01
loss_scale = 64.0

alpha = (1.0 / (root_coef * cubic_coef)) ** (1.0 / 3.0)
beta = root_coef * alpha

AXES = ("lat", "lon")
F32, BF16 = jnp.float32, jnp.bfloat16
VMEM = pl.BlockSpec(memory_space=pltpu.VMEM)
SMEM = pl.BlockSpec(memory_space=pltpu.SMEM)
HBM = pl.BlockSpec(memory_space=pl.ANY)
UNROLL = 2
TILES = 168


def three_parts(x):
    high = x.astype(BF16)
    rest = x - high.astype(F32)
    mid = rest.astype(BF16)
    return (high, mid, (rest - mid.astype(F32)).astype(BF16))


def pick(sel, x, dims):
    return sum(
        lax.dot_general(sel, part, (dims, ((), ())), preferred_element_type=F32)
        for part in three_parts(x)
    )


def columns(rows):
    n = rows.shape[1]
    eye = lax.broadcasted_iota(jnp.int32, (n, n), 0) == lax.broadcasted_iota(jnp.int32, (n, n), 1)
    eye = jnp.where(eye, 1.0, 0.0).astype(BF16)
    rows = jnp.concatenate([rows.astype(F32)] * 4, axis=0).astype(BF16)
    dims = (((1,), (1,)), ((), ()))
    return lax.dot_general(eye, rows, dims, preferred_element_type=F32).astype(jnp.int32)


def selectors(owner):
    n = owner.shape[0]
    devices = lax.broadcasted_iota(jnp.int32, (n, 128), 1)
    hit = [(owner[:, e : e + 1] == devices) for e in range(2)]
    both = jnp.where(hit[0] | hit[1], 1.0, 0.0).astype(BF16)
    before = lax.broadcasted_iota(jnp.int32, (n, n), 0) > lax.broadcasted_iota(
        jnp.int32, (n, n), 1
    )
    before = jnp.where(before, 1.0, 0.0).astype(BF16)
    rank = jnp.dot(before, both, preferred_element_type=F32)
    return [
        [jnp.where(hit[e] & (rank == k), 1.0, 0.0) for e in range(2)] for k in range(2)
    ]


def ones_before(entry):
    first = lax.broadcasted_iota(jnp.int32, (128, 128), 0)
    second = lax.broadcasted_iota(jnp.int32, (128, 128), 1)
    tri = jnp.where(first < second, 1.0, 0.0).astype(BF16)
    mine = jnp.where(entry == 1, 1.0, 0.0).astype(BF16)
    return jnp.dot(mine, tri, preferred_element_type=F32).astype(jnp.int32)


def pack(owner, local, entry, offset, frac, value, weight, out):
    sel = selectors(columns(owner[...]))
    off = offset[...]
    row = lax.shift_right_logical(off * 37, 8)
    col = off - row * 7
    fields = [frac[:, 0, :] + row.astype(F32), frac[:, 1, :] + col.astype(F32)]
    fields += [value[...], weight[...]]
    where = entry[...]
    lane = lax.broadcasted_iota(jnp.int32, where.shape, 1)
    one = ones_before(where)
    loc = columns(local[...]).astype(F32) + 1.0
    data, names = [], []
    for e in range(2):
        gap = one if e == 0 else lane - one
        word = jnp.where(where == e, (1 << 20) + gap * 256 + lane, 0)
        for k in range(7):
            come = pltpu.roll(word, 128 - (1 << k), 1)
            stay = jnp.where((word & (256 << k)) == 0, word, 0)
            word = jnp.where((come & (256 << k)) != 0, come, stay)
        source = word & 127
        used = word >= (1 << 20)
        moved = [jnp.take_along_axis(x, source, axis=1) for x in fields]
        moved[3] = jnp.where(used, moved[3], 0.0)
        data.append(jnp.concatenate(moved, axis=1))
        count = jnp.sum(jnp.where(used, 1.0, 0.0), axis=1, keepdims=True)
        names.append(jnp.where(lane < 2, loc[:, e : e + 1], count))
    data = jnp.concatenate(data, axis=0)
    names = jnp.concatenate(names, axis=0).astype(BF16)
    got = []
    for k in range(2):
        two = jnp.concatenate(sel[k], axis=0).astype(BF16)
        rows = pick(two, data, ((0,), (0,)))
        for f in range(4):
            out[:, 4 * k + f, :] = rows[:, f * 128 : (f + 1) * 128]
        got.append(
            lax.dot_general(two, names, (((0,), (0,)), ((), ())), preferred_element_type=F32)
        )
    lane = lax.broadcasted_iota(jnp.int32, (128, 128), 1)
    out[:, 8, :] = jnp.where((lane & 1) == 0, got[0], got[1])


def tiling(named, n_patch):
    flat = named.T
    name_c = jnp.concatenate([named[:, k : k + 1] for k in range(2)], axis=0)
    name_r = jnp.concatenate([flat[k : k + 1] for k in range(2)], axis=1)
    size_r = jnp.concatenate([flat[2 + k : 3 + k] for k in range(2)], axis=1)
    size_b = jnp.broadcast_to(size_r, (16, 256)).astype(BF16)

    def flag(x):
        return jnp.where(x, 1.0, 0.0).astype(BF16)

    def iota(shape, axis):
        return lax.broadcasted_iota(jnp.int32, shape, axis)

    earlier = flag((name_c == name_r) & (iota((256, 256), 0) < iota((256, 256), 1)))
    inside = jnp.dot(size_b, earlier, preferred_element_type=F32)[0:1]
    of_patch = flag(name_c == (iota((256, 128), 1) + 1).astype(F32))
    amount = jnp.dot(size_b, of_patch, preferred_element_type=F32).astype(jnp.int32)
    tiles = lax.shift_right_logical(amount + 255, 8).astype(F32)
    below = flag(iota((128, 128), 0) < iota((128, 128), 1))
    first = jnp.dot(tiles.astype(BF16), below, preferred_element_type=F32)
    spread = flag((iota((128, 256), 0) + 1).astype(F32) == name_r)
    start = jnp.dot(first.astype(BF16), spread, preferred_element_type=F32)[0:1]
    ends = jnp.broadcast_to((first + tiles)[0:1], (128, 128)).T
    ends = jnp.concatenate([ends, ends], axis=1)
    owner = jnp.sum(
        jnp.where(ends <= iota((128, 256), 1).astype(F32), 1.0, 0.0), axis=0, keepdims=True
    )
    owner = jnp.minimum(owner, n_patch - 1.0)
    whole = jnp.broadcast_to(jnp.sum(tiles[0:1], axis=1, keepdims=True), (1, 256))
    rows = [start * 256.0 + inside, size_r, owner, whole]
    return jnp.concatenate(rows + rows, axis=0).astype(jnp.int32)


def send_kernel(
    owner,
    local,
    entry,
    offset,
    frac,
    value,
    weight,
    latent_hbm,
    w_hidden,
    recv,
    meta,
    left_hbm,
    latent,
    left,
    sent,
    w_t,
    send_sem,
    recv_sem,
    latent_sem,
    left_sem,
):
    fetch = pltpu.make_async_copy(latent_hbm, latent, latent_sem)
    fetch.start()
    lat_size, lon_size = lax.axis_size("lat"), lax.axis_size("lon")
    n_dev = lat_size * lon_size
    me = lax.axis_index("lat") * lon_size + lax.axis_index("lon")
    mesh_id = pl.DeviceIdType.MESH

    def place(i):
        j = lax.rem(me + i, n_dev)
        return j, (lax.div(j, lon_size), lax.rem(j, lon_size))

    barrier = pltpu.get_barrier_semaphore()

    def greet(i, c):
        pl.semaphore_signal(barrier, inc=1, device_id=place(i)[1], device_id_type=mesh_id)
        return c

    lax.fori_loop(1, n_dev, greet, 0)
    pack(owner, local, entry, offset, frac, value, weight, sent)
    pl.semaphore_wait(barrier, n_dev - 1)

    def send(i, c):
        j, there = place(i)
        pltpu.make_async_remote_copy(
            src_ref=sent.at[j],
            dst_ref=recv.at[me],
            send_sem=send_sem,
            recv_sem=recv_sem,
            device_id=there,
            device_id_type=mesh_id,
        ).start()
        return c

    lax.fori_loop(1, n_dev, send, 0)
    recv[me] = sent[me]

    w_t[...] = w_hidden[...].astype(F32).T.astype(BF16)
    lane = lax.broadcasted_iota(jnp.int32, (256, 128), 1)

    def leave(p, j):
        return pltpu.make_async_copy(left.at[j], left_hbm.at[p], left_sem.at[j])

    fetch.wait()

    def project(i, c):
        for j in range(2):
            p = 2 * i + j

            @pl.when(i > 0)
            def _():
                leave(p - 2, j).wait()

            for m in range(2):
                rows = latent[p, :, m * 256 : (m + 1) * 256]
                full = lax.dot_general(
                    w_t[...],
                    jnp.concatenate([rows, rows], axis=0),
                    (((1,), (1,)), ((), ())),
                    preferred_element_type=F32,
                ) * (1.0 / alpha)
                high = full.astype(BF16)
                low = (full - high.astype(F32)).astype(BF16)
                left[j, m * 256 : (m + 1) * 256, :] = jnp.where(lane < 64, high, low)
            leave(p, j).start()
        return c

    n_patch = latent.shape[0]
    lax.fori_loop(0, n_patch // 2, project, 0)
    for j in range(2):
        leave(n_patch - 2 + j, j).wait()
    pltpu.make_async_remote_copy(
        src_ref=sent.at[pl.ds(0, n_dev - 1)],
        dst_ref=recv.at[pl.ds(0, n_dev - 1)],
        send_sem=send_sem,
        recv_sem=recv_sem,
        device_id=place(1)[1],
        device_id_type=mesh_id,
    ).wait()
    meta[...] = tiling(recv[:, 8, :], latent.shape[0])


def compute_kernel(
    meta,
    left_hbm,
    recv,
    w_hidden,
    b_hidden,
    w_out,
    grad,
    score,
    left,
    total,
    w_t,
    bias,
    head,
    comp,
    dense,
    ready,
    left_sem,
    grad_sem,
    *bufs,
):
    n_patch = left.shape[0]
    n_dev = recv.shape[0]
    derivs, pres, spreads, backs = (bufs[i * UNROLL : (i + 1) * UNROLL] for i in range(4))
    lane = lax.broadcasted_iota(jnp.int32, (256, 128), 1)
    lane4 = lax.broadcasted_iota(jnp.int32, (4, 128), 1)
    lane1 = lax.broadcasted_iota(jnp.int32, (1, 128), 1)

    fetch = pltpu.make_async_copy(left_hbm, left, left_sem)
    fetch.start()
    n_tile = meta[3, 0]

    def tile_of(i):
        return meta[2, i]

    comp[...] = jnp.zeros(comp.shape, F32)
    dense[...] = jnp.zeros(dense.shape, F32)

    def append(i, c):
        for j in range(8):
            s = 8 * i + j
            rows = recv[s, 0:8, :]
            for k in range(2):
                base, n = meta[0, 128 * k + s], meta[1, 128 * k + s]
                half, shift = lax.shift_right_logical(base, 7), base & 127
                turned = pltpu.roll(rows[4 * k : 4 * k + 4], shift, 1)
                end = shift + n
                pltpu.store(comp.at[half], turned, mask=(lane4 >= shift) & (lane4 < end))
                pltpu.store(comp.at[half + 1], turned, mask=lane4 < end - 128)
        return c

    lax.fori_loop(0, n_dev // 8, append, 0)

    w_t[...] = w_hidden[...].astype(F32).T.astype(BF16)
    b_parts = three_parts(jnp.broadcast_to(b_hidden[...] * (1.0 / alpha), (128, 256)).T)
    column = jnp.where(
        lane == 0,
        b_parts[0],
        jnp.where(
            lane == 1, b_parts[1], jnp.where(lane == 2, b_parts[2], jnp.zeros_like(b_parts[0]))
        ),
    )
    bias[0:256, :] = column
    bias[256:512, :] = column
    head[...] = jnp.broadcast_to(w_out[...].astype(F32).reshape(1, 256), (128, 256)).T

    def clear(p, c):
        total[p] = jnp.zeros(total.shape[1:], F32)
        return c

    lax.fori_loop(0, n_patch, clear, 0)
    fetch.wait()

    cells = lax.broadcasted_iota(jnp.int32, (8, 256), 0).astype(F32)
    ones = jnp.ones((128, 256), BF16)

    def hidden(i, pre, spread):
        obs = jnp.concatenate([comp[2 * i], comp[2 * i + 1]], axis=1)
        lat = jnp.maximum(1.0 - jnp.abs(obs[0:1] - cells), 0.0)
        lon = jnp.maximum(1.0 - jnp.abs(obs[1:2] - cells), 0.0)
        corner = jnp.concatenate([lat[r : r + 1] * lon for r in range(8)], axis=0)
        spread[...] = corner
        corner_b = corner.astype(BF16)
        right = jnp.concatenate([corner_b, corner_b, ones], axis=0)
        lhs = jnp.concatenate([left[tile_of(i)], bias[...]], axis=1)
        pre[...] = jnp.dot(lhs, right, preferred_element_type=F32)

    def gelu(i, pre, deriv):
        pred = []
        for m in range(2):
            acc = jnp.zeros((8, 256), F32)
            for q in range(4):
                at = m * 256 + q * 64
                v = pre[at : at + 64, :]
                v2 = v * v
                u = jnp.tanh(v * (v2 + beta))
                h = 1.0 + u
                v_b, w_b, h_b = v.astype(BF16), (1.0 - u).astype(BF16), h.astype(BF16)
                slope = v_b * (v_b * v_b + BF16(beta / 3.0))
                deriv[at : at + 64, :] = h_b * (BF16(1.0 / 3.0) + w_b * slope)
                wo = head[q * 64 : q * 64 + 64, :]
                act = v * h * jnp.concatenate([wo, wo], axis=1)
                acc = acc + jnp.sum(act.reshape(8, 8, 256), axis=0)
            pred.append(jnp.sum(acc, axis=0, keepdims=True) * (0.5 * alpha))
        return pred

    def loss(i, pred):
        obs = jnp.concatenate([comp[2 * i], comp[2 * i + 1]], axis=1)
        value = obs[2:3]
        wts = obs[3:4]
        e0, e1, between = pred[0] - value, pred[1] - value, pred[0] - pred[1]
        s0, s1, sm = (x * x + smooth_sq for x in (e0, e1, between))
        r0, r1, rm = (lax.rsqrt(x) for x in (s0, s1, sm))
        pen = wts * (0.5 * (s0 * r0 + s1 * r1) - 0.5 * (sm * rm))
        mid = between * rm
        scaled = (0.5 * loss_scale) * wts
        return scaled * (e0 * r0 - mid), scaled * (e1 * r1 + mid), pen

    def keep(i, pen):
        dense[pl.ds(2 * i + 2, 1), :] = pen[:, :128]
        dense[pl.ds(2 * i + 3, 1), :] = pen[:, 128:]

    def make_back(spread, g, back):
        corner = spread[...]
        back[...] = jnp.concatenate([corner * g[0], corner * g[1]], axis=0).astype(BF16)

    def backward(i, back, deriv):
        both = lax.dot_general(
            deriv[...], back[...], (((1,), (1,)), ((), ())), preferred_element_type=F32
        )
        total[tile_of(jnp.maximum(i, 0))] += jnp.where(lane < 64, both[0:256], both[256:512])

    def some_tiles(i, pen):
        base = i * UNROLL
        for j in range(UNROLL):
            after, prev = (j + 1) % UNROLL, (j + UNROLL - 1) % UNROLL
            hidden(base + j + 1, pres[after], spreads[after])
            pred = gelu(base + j, pres[j], derivs[j])
            keep(base + j - 1, pen)
            backward(base + j - 1, backs[prev], derivs[prev])
            g0, g1, pen = loss(base + j, pred)
            make_back(spreads[j], (g0, g1), backs[j])
        return pen

    hidden(0, pres[0], spreads[0])
    backs[UNROLL - 1][...] = jnp.zeros((128, 256), BF16)
    derivs[UNROLL - 1][...] = jnp.zeros((512, 256), BF16)
    steps = lax.div(n_tile + UNROLL - 1, UNROLL)
    pen = lax.fori_loop(0, steps, some_tiles, jnp.zeros((1, 256), F32))
    keep(steps * UNROLL - 1, pen)
    backward(steps * UNROLL - 1, backs[UNROLL - 1], derivs[UNROLL - 1])

    def give(i, c):
        for j in range(8):
            s = 8 * i + j
            for k in range(2):
                base = meta[0, 128 * k + s]
                half, shift = lax.shift_right_logical(base, 7), base & 127
                row = jnp.where(
                    lane1 >= shift, dense[pl.ds(half + 2, 1), :], dense[pl.ds(half + 3, 1), :]
                )
                score[pl.ds(2 * s + k, 1), :] = pltpu.roll(row, (128 - shift) & 127, 1)
        return c

    lax.fori_loop(0, n_dev // 8, give, 0)

    def leave(p, j):
        return pltpu.make_async_copy(ready.at[j], grad.at[p], grad_sem.at[j])

    def finish(i, c):
        for j in range(2):
            p = 2 * i + j
            both = total[p] * (1.5 * head[...])
            high = both.astype(BF16)
            low = (both - high.astype(F32)).astype(BF16)
            dims = (((0,), (0,)), ((), ()))
            res = lax.dot_general(high, w_t[...], dims, preferred_element_type=F32)
            res = res + lax.dot_general(low, w_t[...], dims, preferred_element_type=F32)

            @pl.when(i > 0)
            def _():
                leave(p - 2, j).wait()

            ready[j, :, 0:256] = res[0:64]
            ready[j, :, 256:512] = res[64:128]
            leave(p, j).start()
        return c

    lax.fori_loop(0, n_patch // 2, finish, 0)
    for j in range(2):
        leave(n_patch - 2 + j, j).wait()


def unpack_kernel(owner, entry, back, out):
    sel = selectors(columns(owner[...]))
    where = entry[...]
    lane = lax.broadcasted_iota(jnp.int32, where.shape, 1)
    one = ones_before(where)
    got = []
    for e in range(2):
        rows = sum(pick(sel[k][e].astype(BF16), back[:, k, :], ((1,), (0,))) for k in range(2))
        got.append(jnp.take_along_axis(rows, one if e == 1 else lane - one, axis=1))
    out[...] = jnp.where(where == 0, got[0], got[1])


def send(patch_owner, patch_local, obs_patch, cell_offset, frac, obs_value, obs_weight, latent, w_hidden):
    n_patch = latent.shape[0]
    return pl.pallas_call(
        send_kernel,
        out_shape=(
            jax.ShapeDtypeStruct((128, 9, 128), F32),
            jax.ShapeDtypeStruct((8, 256), jnp.int32),
            jax.ShapeDtypeStruct((n_patch, 512, 128), BF16),
        ),
        in_specs=[VMEM] * 7 + [HBM, VMEM],
        out_specs=(VMEM, VMEM, HBM),
        scratch_shapes=[
            pltpu.VMEM(latent.shape, BF16),
            pltpu.VMEM((2, 512, 128), BF16),
            pltpu.VMEM((128, 9, 128), F32),
            pltpu.VMEM((256, 256), BF16),
            pltpu.SemaphoreType.DMA,
            pltpu.SemaphoreType.DMA,
            pltpu.SemaphoreType.DMA,
            pltpu.SemaphoreType.DMA((2,)),
        ],
        compiler_params=pltpu.CompilerParams(
            vmem_limit_bytes=60 * 1024 * 1024, collective_id=0, has_side_effects=True
        ),
    )(patch_owner, patch_local, obs_patch, cell_offset, frac, obs_value, obs_weight, latent, w_hidden)


def compute(meta, left, recv, w_hidden, b_hidden, w_out):
    n_patch = left.shape[0]
    return pl.pallas_call(
        compute_kernel,
        out_shape=(
            jax.ShapeDtypeStruct((n_patch, 64, 512), F32),
            jax.ShapeDtypeStruct((256, 128), F32),
        ),
        in_specs=[SMEM, HBM] + [VMEM] * 4,
        out_specs=(HBM, VMEM),
        scratch_shapes=[
            pltpu.VMEM(left.shape, BF16),
            pltpu.VMEM((n_patch, 256, 128), F32),
            pltpu.VMEM((256, 256), BF16),
            pltpu.VMEM((512, 128), BF16),
            pltpu.VMEM((256, 128), F32),
            pltpu.VMEM((2 * TILES, 4, 128), F32),
            pltpu.VMEM((2 * TILES + 8, 128), F32),
            pltpu.VMEM((2, 64, 512), F32),
            pltpu.SemaphoreType.DMA,
            pltpu.SemaphoreType.DMA((2,)),
        ]
        + [pltpu.VMEM((512, 256), BF16)] * UNROLL
        + [pltpu.VMEM((512, 256), F32)] * UNROLL
        + [pltpu.VMEM((64, 256), F32)] * UNROLL
        + [pltpu.VMEM((128, 256), BF16)] * UNROLL,
        compiler_params=pltpu.CompilerParams(vmem_limit_bytes=60 * 1024 * 1024),
    )(meta, left, recv, w_hidden, b_hidden.reshape(1, 256), w_out)


def unpack(patch_owner, obs_patch, back):
    return pl.pallas_call(
        unpack_kernel,
        out_shape=jax.ShapeDtypeStruct(obs_patch.shape, F32),
        in_specs=[VMEM] * 3,
        out_specs=VMEM,
        compiler_params=pltpu.CompilerParams(vmem_limit_bytes=60 * 1024 * 1024),
    )(patch_owner, obs_patch, back)


def per_device(
    latent,
    patch_owner,
    patch_local,
    obs_patch,
    cell_offset,
    frac,
    obs_value,
    obs_weight,
    w_hidden,
    b_hidden,
    w_out,
):
    recv, meta, left = send(
        patch_owner.T, patch_local.T, obs_patch, cell_offset, frac, obs_value, obs_weight, latent, w_hidden
    )
    grad, score = compute(meta, left, recv, w_hidden, b_hidden, w_out)
    back = lax.all_to_all(score.reshape(128, 2, 128), AXES, 0, 0, tiled=True)
    return (grad, unpack(patch_owner.T, obs_patch, back))


def solution(mesh):
    rows2 = P(AXES, None)
    rows3 = P(AXES, None, None)
    return jax.shard_map(
        per_device,
        mesh=mesh,
        in_specs=(rows3, rows2, rows2, rows2, rows2, rows3, rows2, rows2, P(), P(), P()),
        out_specs=(rows3, rows2),
        check_vma=False,
    )
```

```python
import jax
import jax.numpy as jnp
from jax import lax
from jax.experimental import pallas as pl
from jax.experimental.pallas import tpu as pltpu
from jax.sharding import PartitionSpec as P

root_coef = 0.7978845608028654
cubic_coef = 0.044715
smooth_sq = 0.01
loss_scale = 64.0

alpha = (1.0 / (root_coef * cubic_coef)) ** (1.0 / 3.0)
beta = root_coef * alpha

AXES = ("lat", "lon")
F32, BF16 = jnp.float32, jnp.bfloat16
VMEM = pl.BlockSpec(memory_space=pltpu.VMEM)
SMEM = pl.BlockSpec(memory_space=pltpu.SMEM)
HBM = pl.BlockSpec(memory_space=pl.ANY)
UNROLL = 2
TILES = 168


def three_parts(x):
    high = x.astype(BF16)
    rest = x - high.astype(F32)
    mid = rest.astype(BF16)
    return (high, mid, (rest - mid.astype(F32)).astype(BF16))


def pick(sel, x, dims):
    return sum(
        lax.dot_general(sel, part, (dims, ((), ())), preferred_element_type=F32)
        for part in three_parts(x)
    )


def columns(rows):
    n = rows.shape[1]
    eye = lax.broadcasted_iota(jnp.int32, (n, n), 0) == lax.broadcasted_iota(jnp.int32, (n, n), 1)
    eye = jnp.where(eye, 1.0, 0.0).astype(BF16)
    rows = jnp.concatenate([rows.astype(F32)] * 4, axis=0).astype(BF16)
    dims = (((1,), (1,)), ((), ()))
    return lax.dot_general(eye, rows, dims, preferred_element_type=F32).astype(jnp.int32)


def selectors(owner):
    n = owner.shape[0]
    devices = lax.broadcasted_iota(jnp.int32, (n, 128), 1)
    hit = [(owner[:, e : e + 1] == devices) for e in range(2)]
    both = jnp.where(hit[0] | hit[1], 1.0, 0.0).astype(BF16)
    before = lax.broadcasted_iota(jnp.int32, (n, n), 0) > lax.broadcasted_iota(
        jnp.int32, (n, n), 1
    )
    before = jnp.where(before, 1.0, 0.0).astype(BF16)
    rank = jnp.dot(before, both, preferred_element_type=F32)
    return [
        [jnp.where(hit[e] & (rank == k), 1.0, 0.0) for e in range(2)] for k in range(2)
    ]


def ones_before(entry):
    first = lax.broadcasted_iota(jnp.int32, (128, 128), 0)
    second = lax.broadcasted_iota(jnp.int32, (128, 128), 1)
    tri = jnp.where(first < second, 1.0, 0.0).astype(BF16)
    mine = jnp.where(entry == 1, 1.0, 0.0).astype(BF16)
    return jnp.dot(mine, tri, preferred_element_type=F32).astype(jnp.int32)


def pack(owner, local, entry, offset, frac, value, weight, out):
    sel = selectors(columns(owner[...]))
    off = offset[...]
    row = lax.shift_right_logical(off * 37, 8)
    col = off - row * 7
    fields = [frac[:, 0, :] + row.astype(F32), frac[:, 1, :] + col.astype(F32)]
    fields += [value[...], weight[...]]
    where = entry[...]
    lane = lax.broadcasted_iota(jnp.int32, where.shape, 1)
    one = ones_before(where)
    loc = columns(local[...]).astype(F32) + 1.0
    data, names = [], []
    for e in range(2):
        gap = one if e == 0 else lane - one
        word = jnp.where(where == e, (1 << 20) + gap * 256 + lane, 0)
        for k in range(7):
            come = pltpu.roll(word, 128 - (1 << k), 1)
            stay = jnp.where((word & (256 << k)) == 0, word, 0)
            word = jnp.where((come & (256 << k)) != 0, come, stay)
        source = word & 127
        used = word >= (1 << 20)
        moved = [jnp.take_along_axis(x, source, axis=1) for x in fields]
        moved[3] = jnp.where(used, moved[3], 0.0)
        data.append(jnp.concatenate(moved, axis=1))
        count = jnp.sum(jnp.where(used, 1.0, 0.0), axis=1, keepdims=True)
        names.append(jnp.where(lane < 2, loc[:, e : e + 1], count))
    data = jnp.concatenate(data, axis=0)
    names = jnp.concatenate(names, axis=0).astype(BF16)
    got = []
    for k in range(2):
        two = jnp.concatenate(sel[k], axis=0).astype(BF16)
        rows = pick(two, data, ((0,), (0,)))
        for f in range(4):
            out[:, 4 * k + f, :] = rows[:, f * 128 : (f + 1) * 128]
        got.append(
            lax.dot_general(two, names, (((0,), (0,)), ((), ())), preferred_element_type=F32)
        )
    lane = lax.broadcasted_iota(jnp.int32, (128, 128), 1)
    out[:, 8, :] = jnp.where((lane & 1) == 0, got[0], got[1])


def tiling(named, n_patch):
    flat = named.T
    name_c = jnp.concatenate([named[:, k : k + 1] for k in range(2)], axis=0)
    name_r = jnp.concatenate([flat[k : k + 1] for k in range(2)], axis=1)
    size_r = jnp.concatenate([flat[2 + k : 3 + k] for k in range(2)], axis=1)
    size_b = jnp.broadcast_to(size_r, (16, 256)).astype(BF16)

    def flag(x):
        return jnp.where(x, 1.0, 0.0).astype(BF16)

    def iota(shape, axis):
        return lax.broadcasted_iota(jnp.int32, shape, axis)

    earlier = flag((name_c == name_r) & (iota((256, 256), 0) < iota((256, 256), 1)))
    inside = jnp.dot(size_b, earlier, preferred_element_type=F32)[0:1]
    of_patch = flag(name_c == (iota((256, 128), 1) + 1).astype(F32))
    amount = jnp.dot(size_b, of_patch, preferred_element_type=F32).astype(jnp.int32)
    tiles = lax.shift_right_logical(amount + 255, 8).astype(F32)
    below = flag(iota((128, 128), 0) < iota((128, 128), 1))
    first = jnp.dot(tiles.astype(BF16), below, preferred_element_type=F32)
    spread = flag((iota((128, 256), 0) + 1).astype(F32) == name_r)
    start = jnp.dot(first.astype(BF16), spread, preferred_element_type=F32)[0:1]
    ends = jnp.broadcast_to((first + tiles)[0:1], (128, 128)).T
    ends = jnp.concatenate([ends, ends], axis=1)
    owner = jnp.sum(
        jnp.where(ends <= iota((128, 256), 1).astype(F32), 1.0, 0.0), axis=0, keepdims=True
    )
    owner = jnp.minimum(owner, n_patch - 1.0)
    whole = jnp.broadcast_to(jnp.sum(tiles[0:1], axis=1, keepdims=True), (1, 256))
    rows = [start * 256.0 + inside, size_r, owner, whole]
    return jnp.concatenate(rows + rows, axis=0).astype(jnp.int32)


def send_kernel(
    owner,
    local,
    entry,
    offset,
    frac,
    value,
    weight,
    latent_hbm,
    w_hidden,
    recv,
    meta,
    left_hbm,
    latent,
    left,
    sent,
    w_t,
    send_sem,
    recv_sem,
    latent_sem,
    left_sem,
):
    fetch = pltpu.make_async_copy(latent_hbm, latent, latent_sem)
    fetch.start()
    lat_size, lon_size = lax.axis_size("lat"), lax.axis_size("lon")
    n_dev = lat_size * lon_size
    me = lax.axis_index("lat") * lon_size + lax.axis_index("lon")
    mesh_id = pl.DeviceIdType.MESH

    def place(i):
        j = lax.rem(me + i, n_dev)
        return j, (lax.div(j, lon_size), lax.rem(j, lon_size))

    barrier = pltpu.get_barrier_semaphore()

    def greet(i, c):
        pl.semaphore_signal(barrier, inc=1, device_id=place(i)[1], device_id_type=mesh_id)
        return c

    lax.fori_loop(1, n_dev, greet, 0)
    pack(owner, local, entry, offset, frac, value, weight, sent)
    pl.semaphore_wait(barrier, n_dev - 1)

    def send(i, c):
        j, there = place(i)
        pltpu.make_async_remote_copy(
            src_ref=sent.at[j],
            dst_ref=recv.at[me],
            send_sem=send_sem,
            recv_sem=recv_sem,
            device_id=there,
            device_id_type=mesh_id,
        ).start()
        return c

    lax.fori_loop(1, n_dev, send, 0)
    recv[me] = sent[me]

    w_t[...] = w_hidden[...].astype(F32).T.astype(BF16)
    lane = lax.broadcasted_iota(jnp.int32, (256, 128), 1)

    def leave(p):
        return pltpu.make_async_copy(left.at[p], left_hbm.at[p], left_sem)

    fetch.wait()

    def project(i, c):
        for j in range(4):
            p = 4 * i + j
            for m in range(2):
                rows = latent[p, :, m * 256 : (m + 1) * 256]
                full = lax.dot_general(
                    w_t[...],
                    jnp.concatenate([rows, rows], axis=0),
                    (((1,), (1,)), ((), ())),
                    preferred_element_type=F32,
                ) * (1.0 / alpha)
                high = full.astype(BF16)
                low = (full - high.astype(F32)).astype(BF16)
                left[p, m * 256 : (m + 1) * 256, :] = jnp.where(lane < 64, high, low)
            leave(p).start()
        return c

    n_patch = latent.shape[0]
    lax.fori_loop(0, n_patch // 4, project, 0)
    pltpu.make_async_remote_copy(
        src_ref=sent.at[pl.ds(0, n_dev - 1)],
        dst_ref=recv.at[pl.ds(0, n_dev - 1)],
        send_sem=send_sem,
        recv_sem=recv_sem,
        device_id=place(1)[1],
        device_id_type=mesh_id,
    ).wait()
    meta[...] = tiling(recv[:, 8, :], n_patch)
    pltpu.make_async_copy(left, left_hbm, left_sem).wait()


def compute_kernel(
    meta,
    left_hbm,
    recv,
    w_hidden,
    b_hidden,
    w_out,
    grad,
    score,
    left,
    total,
    w_t,
    bias,
    head,
    comp,
    dense,
    ready,
    left_sem,
    grad_sem,
    *bufs,
):
    n_patch = left.shape[0]
    n_dev = recv.shape[0]
    derivs, pres, spreads, backs = (bufs[i * UNROLL : (i + 1) * UNROLL] for i in range(4))
    lane = lax.broadcasted_iota(jnp.int32, (256, 128), 1)
    lane4 = lax.broadcasted_iota(jnp.int32, (4, 128), 1)
    lane1 = lax.broadcasted_iota(jnp.int32, (1, 128), 1)

    fetch = pltpu.make_async_copy(left_hbm, left, left_sem)
    fetch.start()
    n_tile = meta[3, 0]

    def tile_of(i):
        return meta[2, i]

    comp[...] = jnp.zeros(comp.shape, F32)
    dense[...] = jnp.zeros(dense.shape, F32)

    def append(i, c):
        for j in range(8):
            s = 8 * i + j
            rows = recv[s, 0:8, :]
            for k in range(2):
                base, n = meta[0, 128 * k + s], meta[1, 128 * k + s]
                half, shift = lax.shift_right_logical(base, 7), base & 127
                turned = pltpu.roll(rows[4 * k : 4 * k + 4], shift, 1)
                end = shift + n
                pltpu.store(comp.at[half], turned, mask=(lane4 >= shift) & (lane4 < end))
                pltpu.store(comp.at[half + 1], turned, mask=lane4 < end - 128)
        return c

    lax.fori_loop(0, n_dev // 8, append, 0)

    w_t[...] = w_hidden[...].astype(F32).T.astype(BF16)
    b_parts = three_parts(jnp.broadcast_to(b_hidden[...] * (1.0 / alpha), (128, 256)).T)
    column = jnp.where(
        lane == 0,
        b_parts[0],
        jnp.where(
            lane == 1, b_parts[1], jnp.where(lane == 2, b_parts[2], jnp.zeros_like(b_parts[0]))
        ),
    )
    bias[0:256, :] = column
    bias[256:512, :] = column
    head[...] = jnp.broadcast_to(w_out[...].astype(F32).reshape(1, 256), (128, 256)).T

    def clear(p, c):
        total[p] = jnp.zeros(total.shape[1:], F32)
        return c

    lax.fori_loop(0, n_patch, clear, 0)
    fetch.wait()

    cells = lax.broadcasted_iota(jnp.int32, (8, 256), 0).astype(F32)
    ones = jnp.ones((128, 256), BF16)

    def hidden(i, pre, spread):
        obs = jnp.concatenate([comp[2 * i], comp[2 * i + 1]], axis=1)
        lat = jnp.maximum(1.0 - jnp.abs(obs[0:1] - cells), 0.0)
        lon = jnp.maximum(1.0 - jnp.abs(obs[1:2] - cells), 0.0)
        corner = jnp.concatenate([lat[r : r + 1] * lon for r in range(8)], axis=0)
        spread[...] = corner
        corner_b = corner.astype(BF16)
        right = jnp.concatenate([corner_b, corner_b, ones], axis=0)
        lhs = jnp.concatenate([left[tile_of(i)], bias[...]], axis=1)
        pre[...] = jnp.dot(lhs, right, preferred_element_type=F32)

    def gelu(i, pre, deriv):
        pred = []
        for m in range(2):
            acc = jnp.zeros((8, 256), F32)
            for q in range(4):
                at = m * 256 + q * 64
                v = pre[at : at + 64, :]
                v2 = v * v
                u = jnp.tanh(v * (v2 + beta))
                h = 1.0 + u
                v_b, w_b, h_b = v.astype(BF16), (1.0 - u).astype(BF16), h.astype(BF16)
                slope = v_b * (v_b * v_b + BF16(beta / 3.0))
                deriv[at : at + 64, :] = h_b * (BF16(1.0 / 3.0) + w_b * slope)
                wo = head[q * 64 : q * 64 + 64, :]
                act = v * h * jnp.concatenate([wo, wo], axis=1)
                acc = acc + jnp.sum(act.reshape(8, 8, 256), axis=0)
            pred.append(jnp.sum(acc, axis=0, keepdims=True) * (0.5 * alpha))
        return pred

    def loss(i, pred):
        obs = jnp.concatenate([comp[2 * i], comp[2 * i + 1]], axis=1)
        value = obs[2:3]
        wts = obs[3:4]
        e0, e1, between = pred[0] - value, pred[1] - value, pred[0] - pred[1]
        s0, s1, sm = (x * x + smooth_sq for x in (e0, e1, between))
        r0, r1, rm = (lax.rsqrt(x) for x in (s0, s1, sm))
        pen = wts * (0.5 * (s0 * r0 + s1 * r1) - 0.5 * (sm * rm))
        mid = between * rm
        scaled = (0.5 * loss_scale) * wts
        return scaled * (e0 * r0 - mid), scaled * (e1 * r1 + mid), pen

    def keep(i, pen):
        dense[pl.ds(2 * i + 2, 1), :] = pen[:, :128]
        dense[pl.ds(2 * i + 3, 1), :] = pen[:, 128:]

    def make_back(spread, g, back):
        corner = spread[...]
        back[...] = jnp.concatenate([corner * g[0], corner * g[1]], axis=0).astype(BF16)

    def backward(i, back, deriv):
        both = lax.dot_general(
            deriv[...], back[...], (((1,), (1,)), ((), ())), preferred_element_type=F32
        )
        total[tile_of(jnp.maximum(i, 0))] += jnp.where(lane < 64, both[0:256], both[256:512])

    def some_tiles(i, pen):
        base = i * UNROLL
        for j in range(UNROLL):
            after, prev = (j + 1) % UNROLL, (j + UNROLL - 1) % UNROLL
            hidden(base + j + 1, pres[after], spreads[after])
            pred = gelu(base + j, pres[j], derivs[j])
            keep(base + j - 1, pen)
            backward(base + j - 1, backs[prev], derivs[prev])
            g0, g1, pen = loss(base + j, pred)
            make_back(spreads[j], (g0, g1), backs[j])
        return pen

    hidden(0, pres[0], spreads[0])
    backs[UNROLL - 1][...] = jnp.zeros((128, 256), BF16)
    derivs[UNROLL - 1][...] = jnp.zeros((512, 256), BF16)
    steps = lax.div(n_tile + UNROLL - 1, UNROLL)
    pen = lax.fori_loop(0, steps, some_tiles, jnp.zeros((1, 256), F32))
    keep(steps * UNROLL - 1, pen)
    backward(steps * UNROLL - 1, backs[UNROLL - 1], derivs[UNROLL - 1])

    def give(i, c):
        for j in range(8):
            s = 8 * i + j
            for k in range(2):
                base = meta[0, 128 * k + s]
                half, shift = lax.shift_right_logical(base, 7), base & 127
                row = jnp.where(
                    lane1 >= shift, dense[pl.ds(half + 2, 1), :], dense[pl.ds(half + 3, 1), :]
                )
                score[pl.ds(2 * s + k, 1), :] = pltpu.roll(row, (128 - shift) & 127, 1)
        return c

    lax.fori_loop(0, n_dev // 8, give, 0)

    def leave(p):
        return pltpu.make_async_copy(ready.at[p], grad.at[p], grad_sem)

    def finish(i, c):
        for j in range(4):
            p = 4 * i + j
            both = total[p] * (1.5 * head[...])
            high = both.astype(BF16)
            low = (both - high.astype(F32)).astype(BF16)
            dims = (((0,), (0,)), ((), ()))
            res = lax.dot_general(high, w_t[...], dims, preferred_element_type=F32)
            res = res + lax.dot_general(low, w_t[...], dims, preferred_element_type=F32)

            ready[p, :, 0:256] = res[0:64]
            ready[p, :, 256:512] = res[64:128]
            leave(p).start()
        return c

    lax.fori_loop(0, n_patch // 4, finish, 0)
    pltpu.make_async_copy(ready, grad, grad_sem).wait()


def unpack_kernel(owner, entry, back, out):
    sel = selectors(columns(owner[...]))
    where = entry[...]
    lane = lax.broadcasted_iota(jnp.int32, where.shape, 1)
    one = ones_before(where)
    got = []
    for e in range(2):
        rows = sum(pick(sel[k][e].astype(BF16), back[:, k, :], ((1,), (0,))) for k in range(2))
        got.append(jnp.take_along_axis(rows, one if e == 1 else lane - one, axis=1))
    out[...] = jnp.where(where == 0, got[0], got[1])


def send(patch_owner, patch_local, obs_patch, cell_offset, frac, obs_value, obs_weight, latent, w_hidden):
    n_patch = latent.shape[0]
    return pl.pallas_call(
        send_kernel,
        out_shape=(
            jax.ShapeDtypeStruct((128, 9, 128), F32),
            jax.ShapeDtypeStruct((8, 256), jnp.int32),
            jax.ShapeDtypeStruct((n_patch, 512, 128), BF16),
        ),
        in_specs=[VMEM] * 7 + [HBM, VMEM],
        out_specs=(VMEM, VMEM, HBM),
        scratch_shapes=[
            pltpu.VMEM(latent.shape, BF16),
            pltpu.VMEM((latent.shape[0], 512, 128), BF16),
            pltpu.VMEM((128, 9, 128), F32),
            pltpu.VMEM((256, 256), BF16),
            pltpu.SemaphoreType.DMA,
            pltpu.SemaphoreType.DMA,
            pltpu.SemaphoreType.DMA,
            pltpu.SemaphoreType.DMA,
        ],
        compiler_params=pltpu.CompilerParams(
            vmem_limit_bytes=60 * 1024 * 1024, collective_id=0, has_side_effects=True
        ),
    )(patch_owner, patch_local, obs_patch, cell_offset, frac, obs_value, obs_weight, latent, w_hidden)


def compute(meta, left, recv, w_hidden, b_hidden, w_out):
    n_patch = left.shape[0]
    return pl.pallas_call(
        compute_kernel,
        out_shape=(
            jax.ShapeDtypeStruct((n_patch, 64, 512), F32),
            jax.ShapeDtypeStruct((256, 128), F32),
        ),
        in_specs=[SMEM, HBM] + [VMEM] * 4,
        out_specs=(HBM, VMEM),
        scratch_shapes=[
            pltpu.VMEM(left.shape, BF16),
            pltpu.VMEM((n_patch, 256, 128), F32),
            pltpu.VMEM((256, 256), BF16),
            pltpu.VMEM((512, 128), BF16),
            pltpu.VMEM((256, 128), F32),
            pltpu.VMEM((2 * TILES, 4, 128), F32),
            pltpu.VMEM((2 * TILES + 8, 128), F32),
            pltpu.VMEM((n_patch, 64, 512), F32),
            pltpu.SemaphoreType.DMA,
            pltpu.SemaphoreType.DMA,
        ]
        + [pltpu.VMEM((512, 256), BF16)] * UNROLL
        + [pltpu.VMEM((512, 256), F32)] * UNROLL
        + [pltpu.VMEM((64, 256), F32)] * UNROLL
        + [pltpu.VMEM((128, 256), BF16)] * UNROLL,
        compiler_params=pltpu.CompilerParams(vmem_limit_bytes=60 * 1024 * 1024),
    )(meta, left, recv, w_hidden, b_hidden.reshape(1, 256), w_out)


def unpack(patch_owner, obs_patch, back):
    return pl.pallas_call(
        unpack_kernel,
        out_shape=jax.ShapeDtypeStruct(obs_patch.shape, F32),
        in_specs=[VMEM] * 3,
        out_specs=VMEM,
        compiler_params=pltpu.CompilerParams(vmem_limit_bytes=60 * 1024 * 1024),
    )(patch_owner, obs_patch, back)


def per_device(
    latent,
    patch_owner,
    patch_local,
    obs_patch,
    cell_offset,
    frac,
    obs_value,
    obs_weight,
    w_hidden,
    b_hidden,
    w_out,
):
    recv, meta, left = send(
        patch_owner.T, patch_local.T, obs_patch, cell_offset, frac, obs_value, obs_weight, latent, w_hidden
    )
    grad, score = compute(meta, left, recv, w_hidden, b_hidden, w_out)
    back = lax.all_to_all(score.reshape(128, 2, 128), AXES, 0, 0, tiled=True)
    return (grad, unpack(patch_owner.T, obs_patch, back))


def solution(mesh):
    rows2 = P(AXES, None)
    rows3 = P(AXES, None, None)
    return jax.shard_map(
        per_device,
        mesh=mesh,
        in_specs=(rows3, rows2, rows2, rows2, rows2, rows3, rows2, rows2, P(), P(), P()),
        out_specs=(rows3, rows2),
        check_vma=False,
    )
```

```python
import jax
import jax.numpy as jnp
from jax import lax
from jax.experimental import pallas as pl
from jax.experimental.pallas import tpu as pltpu
from jax.sharding import PartitionSpec as P

root_coef = 0.7978845608028654
cubic_coef = 0.044715
smooth_sq = 0.01
loss_scale = 64.0

alpha = (1.0 / (root_coef * cubic_coef)) ** (1.0 / 3.0)
beta = root_coef * alpha

AXES = ("lat", "lon")
F32, BF16 = jnp.float32, jnp.bfloat16
VMEM = pl.BlockSpec(memory_space=pltpu.VMEM)
SMEM = pl.BlockSpec(memory_space=pltpu.SMEM)
HBM = pl.BlockSpec(memory_space=pl.ANY)
UNROLL = 2
TILES = 168


def three_parts(x):
    high = x.astype(BF16)
    rest = x - high.astype(F32)
    mid = rest.astype(BF16)
    return (high, mid, (rest - mid.astype(F32)).astype(BF16))


def pick(sel, x, dims):
    return sum(
        lax.dot_general(sel, part, (dims, ((), ())), preferred_element_type=F32)
        for part in three_parts(x)
    )


def columns(rows):
    n = rows.shape[1]
    eye = lax.broadcasted_iota(jnp.int32, (n, n), 0) == lax.broadcasted_iota(jnp.int32, (n, n), 1)
    eye = jnp.where(eye, 1.0, 0.0).astype(BF16)
    rows = jnp.concatenate([rows.astype(F32)] * 4, axis=0).astype(BF16)
    dims = (((1,), (1,)), ((), ()))
    return lax.dot_general(eye, rows, dims, preferred_element_type=F32).astype(jnp.int32)


def selectors(owner):
    n = owner.shape[0]
    devices = lax.broadcasted_iota(jnp.int32, (n, 128), 1)
    hit = [(owner[:, e : e + 1] == devices) for e in range(2)]
    both = jnp.where(hit[0] | hit[1], 1.0, 0.0).astype(BF16)
    before = lax.broadcasted_iota(jnp.int32, (n, n), 0) > lax.broadcasted_iota(
        jnp.int32, (n, n), 1
    )
    before = jnp.where(before, 1.0, 0.0).astype(BF16)
    rank = jnp.dot(before, both, preferred_element_type=F32)
    return [
        [jnp.where(hit[e] & (rank == k), 1.0, 0.0) for e in range(2)] for k in range(2)
    ]


def ones_before(entry):
    first = lax.broadcasted_iota(jnp.int32, (128, 128), 0)
    second = lax.broadcasted_iota(jnp.int32, (128, 128), 1)
    tri = jnp.where(first < second, 1.0, 0.0).astype(BF16)
    mine = jnp.where(entry == 1, 1.0, 0.0).astype(BF16)
    return jnp.dot(mine, tri, preferred_element_type=F32).astype(jnp.int32)


def pack(owner, local, entry, offset, frac, value, weight, out):
    sel = selectors(columns(owner[...]))
    off = offset[...]
    row = lax.shift_right_logical(off * 37, 8)
    col = off - row * 7
    fields = [frac[:, 0, :] + row.astype(F32), frac[:, 1, :] + col.astype(F32)]
    fields += [value[...], weight[...]]
    where = entry[...]
    lane = lax.broadcasted_iota(jnp.int32, where.shape, 1)
    one = ones_before(where)
    loc = columns(local[...]).astype(F32) + 1.0
    data, names = [], []
    for e in range(2):
        gap = one if e == 0 else lane - one
        word = jnp.where(where == e, (1 << 20) + gap * 256 + lane, 0)
        for k in range(7):
            come = pltpu.roll(word, 128 - (1 << k), 1)
            stay = jnp.where((word & (256 << k)) == 0, word, 0)
            word = jnp.where((come & (256 << k)) != 0, come, stay)
        source = word & 127
        used = word >= (1 << 20)
        moved = [jnp.take_along_axis(x, source, axis=1) for x in fields]
        moved[3] = jnp.where(used, moved[3], 0.0)
        data.append(jnp.concatenate(moved, axis=1))
        count = jnp.sum(jnp.where(used, 1.0, 0.0), axis=1, keepdims=True)
        names.append(jnp.where(lane < 2, loc[:, e : e + 1], count))
    data = jnp.concatenate(data, axis=0)
    names = jnp.concatenate(names, axis=0).astype(BF16)
    got = []
    for k in range(2):
        two = jnp.concatenate(sel[k], axis=0).astype(BF16)
        rows = pick(two, data, ((0,), (0,)))
        for f in range(4):
            out[:, 4 * k + f, :] = rows[:, f * 128 : (f + 1) * 128]
        got.append(
            lax.dot_general(two, names, (((0,), (0,)), ((), ())), preferred_element_type=F32)
        )
    lane = lax.broadcasted_iota(jnp.int32, (128, 128), 1)
    out[:, 8, :] = jnp.where((lane & 1) == 0, got[0], got[1])


def tiling(named, n_patch):
    flat = named.T
    name_c = jnp.concatenate([named[:, k : k + 1] for k in range(2)], axis=0)
    name_r = jnp.concatenate([flat[k : k + 1] for k in range(2)], axis=1)
    size_r = jnp.concatenate([flat[2 + k : 3 + k] for k in range(2)], axis=1)
    size_b = jnp.broadcast_to(size_r, (16, 256)).astype(BF16)

    def flag(x):
        return jnp.where(x, 1.0, 0.0).astype(BF16)

    def iota(shape, axis):
        return lax.broadcasted_iota(jnp.int32, shape, axis)

    earlier = flag((name_c == name_r) & (iota((256, 256), 0) < iota((256, 256), 1)))
    inside = jnp.dot(size_b, earlier, preferred_element_type=F32)[0:1]
    of_patch = flag(name_c == (iota((256, 128), 1) + 1).astype(F32))
    amount = jnp.dot(size_b, of_patch, preferred_element_type=F32).astype(jnp.int32)
    tiles = lax.shift_right_logical(amount + 255, 8).astype(F32)
    below = flag(iota((128, 128), 0) < iota((128, 128), 1))
    first = jnp.dot(tiles.astype(BF16), below, preferred_element_type=F32)
    spread = flag((iota((128, 256), 0) + 1).astype(F32) == name_r)
    start = jnp.dot(first.astype(BF16), spread, preferred_element_type=F32)[0:1]
    ends = jnp.broadcast_to((first + tiles)[0:1], (128, 128)).T
    ends = jnp.concatenate([ends, ends], axis=1)
    owner = jnp.sum(
        jnp.where(ends <= iota((128, 256), 1).astype(F32), 1.0, 0.0), axis=0, keepdims=True
    )
    owner = jnp.minimum(owner, n_patch - 1.0)
    whole = jnp.broadcast_to(jnp.sum(tiles[0:1], axis=1, keepdims=True), (1, 256))
    rows = [start * 256.0 + inside, size_r, owner, whole]
    return jnp.concatenate(rows + rows, axis=0).astype(jnp.int32)


def send_kernel(
    owner,
    local,
    entry,
    offset,
    frac,
    value,
    weight,
    latent_hbm,
    w_hidden,
    recv_hbm,
    meta,
    left_hbm,
    latent,
    left,
    recv,
    sent,
    w_t,
    send_sem,
    recv_sem,
    latent_sem,
    left_sem,
    out_sem,
):
    fetch = pltpu.make_async_copy(latent_hbm, latent, latent_sem)
    fetch.start()
    lat_size, lon_size = lax.axis_size("lat"), lax.axis_size("lon")
    n_dev = lat_size * lon_size
    me = lax.axis_index("lat") * lon_size + lax.axis_index("lon")
    mesh_id = pl.DeviceIdType.MESH

    def place(i):
        j = lax.rem(me + i, n_dev)
        return j, (lax.div(j, lon_size), lax.rem(j, lon_size))

    barrier = pltpu.get_barrier_semaphore()

    def greet(i, c):
        pl.semaphore_signal(barrier, inc=1, device_id=place(i)[1], device_id_type=mesh_id)
        return c

    lax.fori_loop(1, n_dev, greet, 0, unroll=4)
    pack(owner, local, entry, offset, frac, value, weight, sent)
    pl.semaphore_wait(barrier, n_dev - 1)

    def send(i, c):
        j, there = place(i)
        pltpu.make_async_remote_copy(
            src_ref=sent.at[j],
            dst_ref=recv.at[me],
            send_sem=send_sem,
            recv_sem=recv_sem,
            device_id=there,
            device_id_type=mesh_id,
        ).start()
        return c

    lax.fori_loop(1, n_dev, send, 0, unroll=4)
    recv[me] = sent[me]

    w_t[...] = w_hidden[...].astype(F32).T.astype(BF16)
    lane = lax.broadcasted_iota(jnp.int32, (256, 128), 1)

    def leave(p):
        return pltpu.make_async_copy(left.at[p], left_hbm.at[p], left_sem)

    fetch.wait()

    def project(i, c):
        for j in range(4):
            p = 4 * i + j
            for m in range(2):
                rows = latent[p, :, m * 256 : (m + 1) * 256]
                full = lax.dot_general(
                    w_t[...],
                    jnp.concatenate([rows, rows], axis=0),
                    (((1,), (1,)), ((), ())),
                    preferred_element_type=F32,
                ) * (1.0 / alpha)
                high = full.astype(BF16)
                low = (full - high.astype(F32)).astype(BF16)
                left[p, m * 256 : (m + 1) * 256, :] = jnp.where(lane < 64, high, low)
            leave(p).start()
        return c

    n_patch = latent.shape[0]
    lax.fori_loop(0, n_patch // 4, project, 0)
    pltpu.make_async_remote_copy(
        src_ref=sent.at[pl.ds(0, n_dev - 1)],
        dst_ref=recv.at[pl.ds(0, n_dev - 1)],
        send_sem=send_sem,
        recv_sem=recv_sem,
        device_id=place(1)[1],
        device_id_type=mesh_id,
    ).wait()
    leave_recv = pltpu.make_async_copy(recv.at[:, pl.ds(0, 8), :], recv_hbm, out_sem)
    leave_recv.start()
    meta[...] = tiling(recv[:, 8, :], n_patch)
    leave_recv.wait()
    pltpu.make_async_copy(left, left_hbm, left_sem).wait()


def compute_kernel(
    meta,
    left_hbm,
    recv_hbm,
    w_hidden,
    b_hidden,
    w_out,
    grad,
    score,
    left,
    recv,
    total,
    w_t,
    bias,
    head,
    comp,
    dense,
    ready,
    left_sem,
    recv_sem,
    grad_sem,
    *bufs,
):
    n_patch = left.shape[0]
    n_dev = recv.shape[0]
    derivs, pres, spreads, backs = (bufs[i * UNROLL : (i + 1) * UNROLL] for i in range(4))
    lane = lax.broadcasted_iota(jnp.int32, (256, 128), 1)
    lane4 = lax.broadcasted_iota(jnp.int32, (4, 128), 1)
    lane1 = lax.broadcasted_iota(jnp.int32, (1, 128), 1)

    arrive = pltpu.make_async_copy(recv_hbm, recv, recv_sem)
    arrive.start()
    fetch = pltpu.make_async_copy(left_hbm, left, left_sem)
    fetch.start()
    n_tile = meta[3, 0]

    def tile_of(i):
        return meta[2, i]

    comp[...] = jnp.zeros(comp.shape, F32)
    dense[...] = jnp.zeros(dense.shape, F32)

    def append(i, c):
        for j in range(8):
            s = 8 * i + j
            rows = recv[s]
            for k in range(2):
                base, n = meta[0, 128 * k + s], meta[1, 128 * k + s]
                half, shift = lax.shift_right_logical(base, 7), base & 127
                turned = pltpu.roll(rows[4 * k : 4 * k + 4], shift, 1)
                end = shift + n
                pltpu.store(comp.at[half], turned, mask=(lane4 >= shift) & (lane4 < end))
                pltpu.store(comp.at[half + 1], turned, mask=lane4 < end - 128)
        return c

    w_t[...] = w_hidden[...].astype(F32).T.astype(BF16)
    b_parts = three_parts(jnp.broadcast_to(b_hidden[...] * (1.0 / alpha), (128, 256)).T)
    column = jnp.where(
        lane == 0,
        b_parts[0],
        jnp.where(
            lane == 1, b_parts[1], jnp.where(lane == 2, b_parts[2], jnp.zeros_like(b_parts[0]))
        ),
    )
    bias[0:256, :] = column
    bias[256:512, :] = column
    head[...] = jnp.broadcast_to(w_out[...].astype(F32).reshape(1, 256), (128, 256)).T

    def clear(p, c):
        total[p] = jnp.zeros(total.shape[1:], F32)
        return c

    lax.fori_loop(0, n_patch, clear, 0)
    arrive.wait()
    lax.fori_loop(0, n_dev // 8, append, 0)
    fetch.wait()

    cells = lax.broadcasted_iota(jnp.int32, (8, 256), 0).astype(F32)
    ones = jnp.ones((128, 256), BF16)

    def hidden(i, pre, spread):
        obs = jnp.concatenate([comp[2 * i], comp[2 * i + 1]], axis=1)
        lat = jnp.maximum(1.0 - jnp.abs(obs[0:1] - cells), 0.0)
        lon = jnp.maximum(1.0 - jnp.abs(obs[1:2] - cells), 0.0)
        corner = jnp.concatenate([lat[r : r + 1] * lon for r in range(8)], axis=0)
        spread[...] = corner
        corner_b = corner.astype(BF16)
        right = jnp.concatenate([corner_b, corner_b, ones], axis=0)
        lhs = jnp.concatenate([left[tile_of(i)], bias[...]], axis=1)
        pre[...] = jnp.dot(lhs, right, preferred_element_type=F32)

    def gelu(i, pre, deriv):
        pred = []
        for m in range(2):
            acc = jnp.zeros((8, 256), F32)
            for q in range(4):
                at = m * 256 + q * 64
                v = pre[at : at + 64, :]
                v2 = v * v
                u = jnp.tanh(v * (v2 + beta))
                h = 1.0 + u
                v_b, w_b, h_b = v.astype(BF16), (1.0 - u).astype(BF16), h.astype(BF16)
                slope = v_b * (v_b * v_b + BF16(beta / 3.0))
                deriv[at : at + 64, :] = h_b * (BF16(1.0 / 3.0) + w_b * slope)
                wo = head[q * 64 : q * 64 + 64, :]
                act = v * h * jnp.concatenate([wo, wo], axis=1)
                acc = acc + jnp.sum(act.reshape(8, 8, 256), axis=0)
            pred.append(jnp.sum(acc, axis=0, keepdims=True) * (0.5 * alpha))
        return pred

    def loss(i, pred):
        obs = jnp.concatenate([comp[2 * i], comp[2 * i + 1]], axis=1)
        value = obs[2:3]
        wts = obs[3:4]
        e0, e1, between = pred[0] - value, pred[1] - value, pred[0] - pred[1]
        s0, s1, sm = (x * x + smooth_sq for x in (e0, e1, between))
        r0, r1, rm = (lax.rsqrt(x) for x in (s0, s1, sm))
        pen = wts * (0.5 * (s0 * r0 + s1 * r1) - 0.5 * (sm * rm))
        mid = between * rm
        scaled = (0.5 * loss_scale) * wts
        return scaled * (e0 * r0 - mid), scaled * (e1 * r1 + mid), pen

    def keep(i, pen):
        dense[pl.ds(2 * i + 2, 1), :] = pen[:, :128]
        dense[pl.ds(2 * i + 3, 1), :] = pen[:, 128:]

    def make_back(spread, g, back):
        corner = spread[...]
        back[...] = jnp.concatenate([corner * g[0], corner * g[1]], axis=0).astype(BF16)

    def backward(i, back, deriv):
        both = lax.dot_general(
            deriv[...], back[...], (((1,), (1,)), ((), ())), preferred_element_type=F32
        )
        total[tile_of(jnp.maximum(i, 0))] += jnp.where(lane < 64, both[0:256], both[256:512])

    def some_tiles(i, pen):
        base = i * UNROLL
        for j in range(UNROLL):
            after, prev = (j + 1) % UNROLL, (j + UNROLL - 1) % UNROLL
            hidden(base + j + 1, pres[after], spreads[after])
            pred = gelu(base + j, pres[j], derivs[j])
            keep(base + j - 1, pen)
            backward(base + j - 1, backs[prev], derivs[prev])
            g0, g1, pen = loss(base + j, pred)
            make_back(spreads[j], (g0, g1), backs[j])
        return pen

    hidden(0, pres[0], spreads[0])
    backs[UNROLL - 1][...] = jnp.zeros((128, 256), BF16)
    derivs[UNROLL - 1][...] = jnp.zeros((512, 256), BF16)
    steps = lax.div(n_tile + UNROLL - 1, UNROLL)
    pen = lax.fori_loop(0, steps, some_tiles, jnp.zeros((1, 256), F32))
    keep(steps * UNROLL - 1, pen)
    backward(steps * UNROLL - 1, backs[UNROLL - 1], derivs[UNROLL - 1])

    def give(i, c):
        for j in range(8):
            s = 8 * i + j
            for k in range(2):
                base = meta[0, 128 * k + s]
                half, shift = lax.shift_right_logical(base, 7), base & 127
                row = jnp.where(
                    lane1 >= shift, dense[pl.ds(half + 2, 1), :], dense[pl.ds(half + 3, 1), :]
                )
                score[pl.ds(2 * s + k, 1), :] = pltpu.roll(row, (128 - shift) & 127, 1)
        return c

    lax.fori_loop(0, n_dev // 8, give, 0)

    def leave(p):
        return pltpu.make_async_copy(ready.at[p], grad.at[p], grad_sem)

    def finish(i, c):
        for j in range(4):
            p = 4 * i + j
            both = total[p] * (1.5 * head[...])
            high = both.astype(BF16)
            dims = (((0,), (0,)), ((), ()))
            res = lax.dot_general(high, w_t[...], dims, preferred_element_type=F32)

            ready[p, :, 0:256] = res[0:64]
            ready[p, :, 256:512] = res[64:128]
            leave(p).start()
        return c

    lax.fori_loop(0, n_patch // 4, finish, 0)
    pltpu.make_async_copy(ready, grad, grad_sem).wait()


def unpack_kernel(owner, entry, score, out, back, send_sem, recv_sem):
    lat_size, lon_size = lax.axis_size("lat"), lax.axis_size("lon")
    n_dev = lat_size * lon_size
    me = lax.axis_index("lat") * lon_size + lax.axis_index("lon")
    mesh_id = pl.DeviceIdType.MESH

    def place(i):
        j = lax.rem(me + i, n_dev)
        return j, (lax.div(j, lon_size), lax.rem(j, lon_size))

    barrier = pltpu.get_barrier_semaphore()

    def greet(i, c):
        pl.semaphore_signal(barrier, inc=1, device_id=place(i)[1], device_id_type=mesh_id)
        return c

    lax.fori_loop(1, n_dev, greet, 0, unroll=4)
    sel = selectors(columns(owner[...]))
    where = entry[...]
    lane = lax.broadcasted_iota(jnp.int32, where.shape, 1)
    one = ones_before(where)
    pl.semaphore_wait(barrier, n_dev - 1)

    def send_one(i, c):
        j, there = place(i)
        pltpu.make_async_remote_copy(
            src_ref=score.at[j],
            dst_ref=back.at[me],
            send_sem=send_sem,
            recv_sem=recv_sem,
            device_id=there,
            device_id_type=mesh_id,
        ).start()
        return c

    lax.fori_loop(1, n_dev, send_one, 0, unroll=4)
    back[me] = score[me]
    pltpu.make_async_remote_copy(
        src_ref=score.at[pl.ds(0, n_dev - 1)],
        dst_ref=back.at[pl.ds(0, n_dev - 1)],
        send_sem=send_sem,
        recv_sem=recv_sem,
        device_id=place(1)[1],
        device_id_type=mesh_id,
    ).wait()
    got = []
    for e in range(2):
        rows = sum(pick(sel[k][e].astype(BF16), back[:, k, :], ((1,), (0,))) for k in range(2))
        got.append(jnp.take_along_axis(rows, one if e == 1 else lane - one, axis=1))
    out[...] = jnp.where(where == 0, got[0], got[1])


def send(patch_owner, patch_local, obs_patch, cell_offset, frac, obs_value, obs_weight, latent, w_hidden):
    n_patch = latent.shape[0]
    return pl.pallas_call(
        send_kernel,
        out_shape=(
            jax.ShapeDtypeStruct((128, 8, 128), F32),
            jax.ShapeDtypeStruct((8, 256), jnp.int32),
            jax.ShapeDtypeStruct((n_patch, 512, 128), BF16),
        ),
        in_specs=[VMEM] * 7 + [HBM, VMEM],
        out_specs=(HBM, VMEM, HBM),
        scratch_shapes=[
            pltpu.VMEM(latent.shape, BF16),
            pltpu.VMEM((latent.shape[0], 512, 128), BF16),
            pltpu.VMEM((128, 9, 128), F32),
            pltpu.VMEM((128, 9, 128), F32),
            pltpu.VMEM((256, 256), BF16),
            pltpu.SemaphoreType.DMA,
            pltpu.SemaphoreType.DMA,
            pltpu.SemaphoreType.DMA,
            pltpu.SemaphoreType.DMA,
            pltpu.SemaphoreType.DMA,
        ],
        compiler_params=pltpu.CompilerParams(
            vmem_limit_bytes=60 * 1024 * 1024, collective_id=0, has_side_effects=True
        ),
    )(patch_owner, patch_local, obs_patch, cell_offset, frac, obs_value, obs_weight, latent, w_hidden)


def compute(meta, left, recv, w_hidden, b_hidden, w_out):
    n_patch = left.shape[0]
    return pl.pallas_call(
        compute_kernel,
        out_shape=(
            jax.ShapeDtypeStruct((n_patch, 64, 512), F32),
            jax.ShapeDtypeStruct((256, 128), F32),
        ),
        in_specs=[SMEM, HBM, HBM] + [VMEM] * 3,
        out_specs=(HBM, VMEM),
        scratch_shapes=[
            pltpu.VMEM(left.shape, BF16),
            pltpu.VMEM(recv.shape, F32),
            pltpu.VMEM((n_patch, 256, 128), F32),
            pltpu.VMEM((256, 256), BF16),
            pltpu.VMEM((512, 128), BF16),
            pltpu.VMEM((256, 128), F32),
            pltpu.VMEM((2 * TILES, 4, 128), F32),
            pltpu.VMEM((2 * TILES + 8, 128), F32),
            pltpu.VMEM((n_patch, 64, 512), F32),
            pltpu.SemaphoreType.DMA,
            pltpu.SemaphoreType.DMA,
            pltpu.SemaphoreType.DMA,
        ]
        + [pltpu.VMEM((512, 256), BF16)] * UNROLL
        + [pltpu.VMEM((512, 256), F32)] * UNROLL
        + [pltpu.VMEM((64, 256), F32)] * UNROLL
        + [pltpu.VMEM((128, 256), BF16)] * UNROLL,
        compiler_params=pltpu.CompilerParams(vmem_limit_bytes=60 * 1024 * 1024),
    )(meta, left, recv, w_hidden, b_hidden.reshape(1, 256), w_out)


def unpack(patch_owner, obs_patch, score):
    return pl.pallas_call(
        unpack_kernel,
        out_shape=jax.ShapeDtypeStruct(obs_patch.shape, F32),
        in_specs=[VMEM] * 3,
        out_specs=VMEM,
        scratch_shapes=[
            pltpu.VMEM(score.shape, F32),
            pltpu.SemaphoreType.DMA,
            pltpu.SemaphoreType.DMA,
        ],
        compiler_params=pltpu.CompilerParams(
            vmem_limit_bytes=60 * 1024 * 1024, collective_id=1, has_side_effects=True
        ),
    )(patch_owner, obs_patch, score)


def per_device(
    latent,
    patch_owner,
    patch_local,
    obs_patch,
    cell_offset,
    frac,
    obs_value,
    obs_weight,
    w_hidden,
    b_hidden,
    w_out,
):
    recv, meta, left = send(
        patch_owner.T, patch_local.T, obs_patch, cell_offset, frac, obs_value, obs_weight, latent, w_hidden
    )
    grad, score = compute(meta, left, recv, w_hidden, b_hidden, w_out)
    return (grad, unpack(patch_owner.T, obs_patch, score.reshape(128, 2, 128)))


def solution(mesh):
    rows2 = P(AXES, None)
    rows3 = P(AXES, None, None)
    return jax.shard_map(
        per_device,
        mesh=mesh,
        in_specs=(rows3, rows2, rows2, rows2, rows2, rows3, rows2, rows2, P(), P(), P()),
        out_specs=(rows3, rows2),
        check_vma=False,
    )
```

```python
import jax
import jax.numpy as jnp
from jax import lax
from jax.experimental import pallas as pl
from jax.experimental.pallas import tpu as pltpu
from jax.sharding import PartitionSpec as P

root_coef = 0.7978845608028654
cubic_coef = 0.044715
smooth_sq = 0.01
loss_scale = 64.0

alpha = (1.0 / (root_coef * cubic_coef)) ** (1.0 / 3.0)
beta = root_coef * alpha

AXES = ("lat", "lon")
F32, BF16 = jnp.float32, jnp.bfloat16
VMEM = pl.BlockSpec(memory_space=pltpu.VMEM)
SMEM = pl.BlockSpec(memory_space=pltpu.SMEM)
HBM = pl.BlockSpec(memory_space=pl.ANY)
UNROLL = 2
TILES = 168


def three_parts(x):
    high = x.astype(BF16)
    rest = x - high.astype(F32)
    mid = rest.astype(BF16)
    return (high, mid, (rest - mid.astype(F32)).astype(BF16))


def pick(sel, x, dims):
    return sum(
        lax.dot_general(sel, part, (dims, ((), ())), preferred_element_type=F32)
        for part in three_parts(x)
    )


def columns(rows):
    n = rows.shape[1]
    eye = lax.broadcasted_iota(jnp.int32, (n, n), 0) == lax.broadcasted_iota(jnp.int32, (n, n), 1)
    eye = jnp.where(eye, 1.0, 0.0).astype(BF16)
    rows = jnp.concatenate([rows.astype(F32)] * 4, axis=0).astype(BF16)
    dims = (((1,), (1,)), ((), ()))
    return lax.dot_general(eye, rows, dims, preferred_element_type=F32).astype(jnp.int32)


def selectors(owner):
    n = owner.shape[0]
    devices = lax.broadcasted_iota(jnp.int32, (n, 128), 1)
    hit = [(owner[:, e : e + 1] == devices) for e in range(2)]
    both = jnp.where(hit[0] | hit[1], 1.0, 0.0).astype(BF16)
    before = lax.broadcasted_iota(jnp.int32, (n, n), 0) > lax.broadcasted_iota(
        jnp.int32, (n, n), 1
    )
    before = jnp.where(before, 1.0, 0.0).astype(BF16)
    rank = jnp.dot(before, both, preferred_element_type=F32)
    return [
        [jnp.where(hit[e] & (rank == k), 1.0, 0.0) for e in range(2)] for k in range(2)
    ]


def ones_before(entry):
    first = lax.broadcasted_iota(jnp.int32, (128, 128), 0)
    second = lax.broadcasted_iota(jnp.int32, (128, 128), 1)
    tri = jnp.where(first < second, 1.0, 0.0).astype(BF16)
    mine = jnp.where(entry == 1, 1.0, 0.0).astype(BF16)
    return jnp.dot(mine, tri, preferred_element_type=F32).astype(jnp.int32)


def pack(owner, local, entry, offset, frac, value, weight, out):
    sel = selectors(columns(owner[...]))
    off = offset[...]
    row = lax.shift_right_logical(off * 37, 8)
    col = off - row * 7
    fields = [frac[:, 0, :] + row.astype(F32), frac[:, 1, :] + col.astype(F32)]
    fields += [value[...], weight[...]]
    where = entry[...]
    lane = lax.broadcasted_iota(jnp.int32, where.shape, 1)
    one = ones_before(where)
    loc = columns(local[...]).astype(F32) + 1.0
    data, names = [], []
    for e in range(2):
        gap = one if e == 0 else lane - one
        word = jnp.where(where == e, (1 << 20) + gap * 256 + lane, 0)
        for k in range(7):
            come = pltpu.roll(word, 128 - (1 << k), 1)
            stay = jnp.where((word & (256 << k)) == 0, word, 0)
            word = jnp.where((come & (256 << k)) != 0, come, stay)
        source = word & 127
        used = word >= (1 << 20)
        moved = [jnp.take_along_axis(x, source, axis=1) for x in fields]
        moved[3] = jnp.where(used, moved[3], 0.0)
        data.append(jnp.concatenate(moved, axis=1))
        count = jnp.sum(jnp.where(used, 1.0, 0.0), axis=1, keepdims=True)
        names.append(jnp.where(lane < 2, loc[:, e : e + 1], count))
    data = jnp.concatenate(data, axis=0)
    names = jnp.concatenate(names, axis=0).astype(BF16)
    got = []
    for k in range(2):
        two = jnp.concatenate(sel[k], axis=0).astype(BF16)
        rows = pick(two, data, ((0,), (0,)))
        for f in range(4):
            out[:, 4 * k + f, :] = rows[:, f * 128 : (f + 1) * 128]
        got.append(
            lax.dot_general(two, names, (((0,), (0,)), ((), ())), preferred_element_type=F32)
        )
    lane = lax.broadcasted_iota(jnp.int32, (128, 128), 1)
    out[:, 8, :] = jnp.where((lane & 1) == 0, got[0], got[1])


def tiling(named, n_patch):
    flat = named.T
    name_c = jnp.concatenate([named[:, k : k + 1] for k in range(2)], axis=0)
    name_r = jnp.concatenate([flat[k : k + 1] for k in range(2)], axis=1)
    size_r = jnp.concatenate([flat[2 + k : 3 + k] for k in range(2)], axis=1)
    size_b = jnp.broadcast_to(size_r, (16, 256)).astype(BF16)

    def flag(x):
        return jnp.where(x, 1.0, 0.0).astype(BF16)

    def iota(shape, axis):
        return lax.broadcasted_iota(jnp.int32, shape, axis)

    earlier = flag((name_c == name_r) & (iota((256, 256), 0) < iota((256, 256), 1)))
    inside = jnp.dot(size_b, earlier, preferred_element_type=F32)[0:1]
    of_patch = flag(name_c == (iota((256, 128), 1) + 1).astype(F32))
    amount = jnp.dot(size_b, of_patch, preferred_element_type=F32).astype(jnp.int32)
    tiles = lax.shift_right_logical(amount + 255, 8).astype(F32)
    below = flag(iota((128, 128), 0) < iota((128, 128), 1))
    first = jnp.dot(tiles.astype(BF16), below, preferred_element_type=F32)
    spread = flag((iota((128, 256), 0) + 1).astype(F32) == name_r)
    start = jnp.dot(first.astype(BF16), spread, preferred_element_type=F32)[0:1]
    ends = jnp.broadcast_to((first + tiles)[0:1], (128, 128)).T
    ends = jnp.concatenate([ends, ends], axis=1)
    owner = jnp.sum(
        jnp.where(ends <= iota((128, 256), 1).astype(F32), 1.0, 0.0), axis=0, keepdims=True
    )
    owner = jnp.minimum(owner, n_patch - 1.0)
    whole = jnp.broadcast_to(jnp.sum(tiles[0:1], axis=1, keepdims=True), (1, 256))
    rows = [start * 256.0 + inside, size_r, owner, whole]
    return jnp.concatenate(rows + rows, axis=0).astype(jnp.int32)


def send_kernel(
    owner,
    local,
    entry,
    offset,
    frac,
    value,
    weight,
    latent_hbm,
    w_hidden,
    recv_hbm,
    meta,
    left_hbm,
    latent,
    left,
    recv,
    sent,
    w_t,
    send_sem,
    recv_sem,
    latent_sem,
    left_sem,
    out_sem,
):
    fetch = pltpu.make_async_copy(latent_hbm, latent, latent_sem)
    fetch.start()
    lat_size, lon_size = lax.axis_size("lat"), lax.axis_size("lon")
    n_dev = lat_size * lon_size
    me = lax.axis_index("lat") * lon_size + lax.axis_index("lon")
    mesh_id = pl.DeviceIdType.MESH

    def place(i):
        j = lax.rem(me + i, n_dev)
        return j, (lax.div(j, lon_size), lax.rem(j, lon_size))

    barrier = pltpu.get_barrier_semaphore()

    def greet(i, c):
        pl.semaphore_signal(barrier, inc=1, device_id=place(i)[1], device_id_type=mesh_id)
        return c

    lax.fori_loop(1, n_dev, greet, 0, unroll=4)
    pack(owner, local, entry, offset, frac, value, weight, sent)
    pl.semaphore_wait(barrier, n_dev - 1)

    def send(i, c):
        j, there = place(i)
        pltpu.make_async_remote_copy(
            src_ref=sent.at[j],
            dst_ref=recv.at[me],
            send_sem=send_sem,
            recv_sem=recv_sem,
            device_id=there,
            device_id_type=mesh_id,
        ).start()
        return c

    lax.fori_loop(1, n_dev, send, 0, unroll=4)
    recv[me] = sent[me]

    w_t[...] = w_hidden[...].astype(F32).T.astype(BF16)
    lane = lax.broadcasted_iota(jnp.int32, (256, 128), 1)

    def leave(p):
        return pltpu.make_async_copy(left.at[p], left_hbm.at[p], left_sem)

    fetch.wait()

    def project(i, c):
        for j in range(4):
            p = 4 * i + j
            for m in range(2):
                rows = latent[p, :, m * 256 : (m + 1) * 256]
                full = lax.dot_general(
                    w_t[...],
                    jnp.concatenate([rows, rows], axis=0),
                    (((1,), (1,)), ((), ())),
                    preferred_element_type=F32,
                ) * (1.0 / alpha)
                high = full.astype(BF16)
                low = (full - high.astype(F32)).astype(BF16)
                left[p, m * 256 : (m + 1) * 256, :] = jnp.where(lane < 64, high, low)
            leave(p).start()
        return c

    n_patch = latent.shape[0]
    lax.fori_loop(0, n_patch // 4, project, 0)
    pltpu.make_async_remote_copy(
        src_ref=sent.at[pl.ds(0, n_dev - 1)],
        dst_ref=recv.at[pl.ds(0, n_dev - 1)],
        send_sem=send_sem,
        recv_sem=recv_sem,
        device_id=place(1)[1],
        device_id_type=mesh_id,
    ).wait()
    leave_recv = pltpu.make_async_copy(recv.at[:, pl.ds(0, 8), :], recv_hbm, out_sem)
    leave_recv.start()
    meta[...] = tiling(recv[:, 8, :], n_patch)
    leave_recv.wait()
    pltpu.make_async_copy(left, left_hbm, left_sem).wait()


def compute_kernel(
    meta,
    left_hbm,
    recv_hbm,
    w_hidden,
    b_hidden,
    w_out,
    grad,
    score,
    left,
    recv,
    total,
    w_t,
    bias,
    head,
    comp,
    dense,
    ready,
    left_sem,
    recv_sem,
    grad_sem,
    *bufs,
):
    n_patch = left.shape[0]
    n_dev = recv.shape[0]
    derivs, pres, spreads, backs = (bufs[i * UNROLL : (i + 1) * UNROLL] for i in range(4))
    lane = lax.broadcasted_iota(jnp.int32, (256, 128), 1)
    lane4 = lax.broadcasted_iota(jnp.int32, (4, 128), 1)
    lane1 = lax.broadcasted_iota(jnp.int32, (1, 128), 1)

    arrive = pltpu.make_async_copy(recv_hbm, recv, recv_sem)
    arrive.start()
    fetch = pltpu.make_async_copy(left_hbm, left, left_sem)
    fetch.start()
    n_tile = meta[3, 0]

    def tile_of(i):
        return meta[2, i]

    comp[...] = jnp.zeros(comp.shape, F32)
    dense[...] = jnp.zeros(dense.shape, F32)

    def append(i, c):
        for j in range(8):
            s = 8 * i + j
            rows = recv[s]
            for k in range(2):
                base, n = meta[0, 128 * k + s], meta[1, 128 * k + s]
                half, shift = lax.shift_right_logical(base, 7), base & 127
                turned = pltpu.roll(rows[4 * k : 4 * k + 4], shift, 1)
                end = shift + n
                pltpu.store(comp.at[half], turned, mask=(lane4 >= shift) & (lane4 < end))
                pltpu.store(comp.at[half + 1], turned, mask=lane4 < end - 128)
        return c

    w_t[...] = w_hidden[...].astype(F32).T.astype(BF16)
    b_parts = three_parts(jnp.broadcast_to(b_hidden[...] * (1.0 / alpha), (128, 256)).T)
    column = jnp.where(
        lane == 0,
        b_parts[0],
        jnp.where(
            lane == 1, b_parts[1], jnp.where(lane == 2, b_parts[2], jnp.zeros_like(b_parts[0]))
        ),
    )
    bias[0:256, :] = column
    bias[256:512, :] = column
    head[...] = jnp.broadcast_to(w_out[...].astype(F32).reshape(1, 256), (128, 256)).T

    def clear(p, c):
        total[p] = jnp.zeros(total.shape[1:], F32)
        return c

    lax.fori_loop(0, n_patch, clear, 0)
    arrive.wait()
    lax.fori_loop(0, n_dev // 8, append, 0)
    fetch.wait()

    cells = lax.broadcasted_iota(jnp.int32, (8, 256), 0).astype(F32)
    ones = jnp.ones((128, 256), BF16)

    def hidden(i, pre, spread):
        obs = jnp.concatenate([comp[2 * i], comp[2 * i + 1]], axis=1)
        lat = jnp.maximum(1.0 - jnp.abs(obs[0:1] - cells), 0.0)
        lon = jnp.maximum(1.0 - jnp.abs(obs[1:2] - cells), 0.0)
        corner = jnp.concatenate([lat[r : r + 1] * lon for r in range(8)], axis=0)
        spread[...] = corner
        corner_b = corner.astype(BF16)
        right = jnp.concatenate([corner_b, corner_b, ones], axis=0)
        lhs = jnp.concatenate([left[tile_of(i)], bias[...]], axis=1)
        pre[...] = jnp.dot(lhs, right, preferred_element_type=F32)

    def gelu(i, pre, deriv):
        pred = []
        for m in range(2):
            acc = jnp.zeros((8, 256), F32)
            for q in range(4):
                at = m * 256 + q * 64
                v = pre[at : at + 64, :]
                v2 = v * v
                u = jnp.tanh(v * (v2 + beta))
                h = 1.0 + u
                v_b, w_b, h_b = v.astype(BF16), (1.0 - u).astype(BF16), h.astype(BF16)
                slope = v_b * (v_b * v_b + BF16(beta / 3.0))
                deriv[at : at + 64, :] = h_b * (BF16(1.0 / 3.0) + w_b * slope)
                wo = head[q * 64 : q * 64 + 64, :]
                act = v * h * jnp.concatenate([wo, wo], axis=1)
                acc = acc + jnp.sum(act.reshape(8, 8, 256), axis=0)
            pred.append(jnp.sum(acc, axis=0, keepdims=True) * (0.5 * alpha))
        return pred

    def loss(i, pred):
        obs = jnp.concatenate([comp[2 * i], comp[2 * i + 1]], axis=1)
        value = obs[2:3]
        wts = obs[3:4]
        e0, e1, between = pred[0] - value, pred[1] - value, pred[0] - pred[1]
        s0, s1, sm = (x * x + smooth_sq for x in (e0, e1, between))
        r0, r1, rm = (lax.rsqrt(x) for x in (s0, s1, sm))
        pen = wts * (0.5 * (s0 * r0 + s1 * r1) - 0.5 * (sm * rm))
        mid = between * rm
        scaled = (0.5 * loss_scale) * wts
        return scaled * (e0 * r0 - mid), scaled * (e1 * r1 + mid), pen

    def keep(i, pen):
        dense[pl.ds(2 * i + 2, 1), :] = pen[:, :128]
        dense[pl.ds(2 * i + 3, 1), :] = pen[:, 128:]

    def make_back(spread, g, back):
        corner = spread[...]
        back[...] = jnp.concatenate([corner * g[0], corner * g[1]], axis=0).astype(BF16)

    def backward(i, back, deriv):
        both = lax.dot_general(
            deriv[...], back[...], (((1,), (1,)), ((), ())), preferred_element_type=F32
        )
        total[tile_of(jnp.maximum(i, 0))] += jnp.where(lane < 64, both[0:256], both[256:512])

    def some_tiles(i, pen):
        base = i * UNROLL
        for j in range(UNROLL):
            after, prev = (j + 1) % UNROLL, (j + UNROLL - 1) % UNROLL
            hidden(base + j + 1, pres[after], spreads[after])
            pred = gelu(base + j, pres[j], derivs[j])
            keep(base + j - 1, pen)
            backward(base + j - 1, backs[prev], derivs[prev])
            g0, g1, pen = loss(base + j, pred)
            make_back(spreads[j], (g0, g1), backs[j])
        return pen

    hidden(0, pres[0], spreads[0])
    backs[UNROLL - 1][...] = jnp.zeros((128, 256), BF16)
    derivs[UNROLL - 1][...] = jnp.zeros((512, 256), BF16)
    steps = lax.div(n_tile + UNROLL - 1, UNROLL)
    pen = lax.fori_loop(0, steps, some_tiles, jnp.zeros((1, 256), F32))
    keep(steps * UNROLL - 1, pen)
    backward(steps * UNROLL - 1, backs[UNROLL - 1], derivs[UNROLL - 1])

    def give(i, c):
        for j in range(8):
            s = 8 * i + j
            for k in range(2):
                base = meta[0, 128 * k + s]
                half, shift = lax.shift_right_logical(base, 7), base & 127
                row = jnp.where(
                    lane1 >= shift, dense[pl.ds(half + 2, 1), :], dense[pl.ds(half + 3, 1), :]
                )
                score[pl.ds(2 * s + k, 1), :] = pltpu.roll(row, (128 - shift) & 127, 1)
        return c

    lax.fori_loop(0, n_dev // 8, give, 0)

    def leave(p):
        return pltpu.make_async_copy(ready.at[p], grad.at[p], grad_sem)

    def finish(i, c):
        for j in range(8):
            p = 8 * i + j
            both = total[p] * (1.5 * head[...])
            high = both.astype(BF16)
            dims = (((0,), (0,)), ((), ()))
            res = lax.dot_general(high, w_t[...], dims, preferred_element_type=F32)

            ready[p, :, 0:256] = res[0:64]
            ready[p, :, 256:512] = res[64:128]
            leave(p).start()
        return c

    lax.fori_loop(0, n_patch // 8, finish, 0)
    pltpu.make_async_copy(ready, grad, grad_sem).wait()


def unpack_kernel(owner, entry, score, out, back, send_sem, recv_sem):
    lat_size, lon_size = lax.axis_size("lat"), lax.axis_size("lon")
    n_dev = lat_size * lon_size
    me = lax.axis_index("lat") * lon_size + lax.axis_index("lon")
    mesh_id = pl.DeviceIdType.MESH

    def place(i):
        j = lax.rem(me + i, n_dev)
        return j, (lax.div(j, lon_size), lax.rem(j, lon_size))

    barrier = pltpu.get_barrier_semaphore()

    def greet(i, c):
        pl.semaphore_signal(barrier, inc=1, device_id=place(i)[1], device_id_type=mesh_id)
        return c

    lax.fori_loop(1, n_dev, greet, 0, unroll=4)
    sel = selectors(columns(owner[...]))
    where = entry[...]
    lane = lax.broadcasted_iota(jnp.int32, where.shape, 1)
    one = ones_before(where)
    pl.semaphore_wait(barrier, n_dev - 1)

    def send_one(i, c):
        j, there = place(i)
        pltpu.make_async_remote_copy(
            src_ref=score.at[j],
            dst_ref=back.at[me],
            send_sem=send_sem,
            recv_sem=recv_sem,
            device_id=there,
            device_id_type=mesh_id,
        ).start()
        return c

    lax.fori_loop(1, n_dev, send_one, 0, unroll=4)
    back[me] = score[me]
    pltpu.make_async_remote_copy(
        src_ref=score.at[pl.ds(0, n_dev - 1)],
        dst_ref=back.at[pl.ds(0, n_dev - 1)],
        send_sem=send_sem,
        recv_sem=recv_sem,
        device_id=place(1)[1],
        device_id_type=mesh_id,
    ).wait()
    got = []
    for e in range(2):
        rows = sum(pick(sel[k][e].astype(BF16), back[:, k, :], ((1,), (0,))) for k in range(2))
        got.append(jnp.take_along_axis(rows, one if e == 1 else lane - one, axis=1))
    out[...] = jnp.where(where == 0, got[0], got[1])


def send(patch_owner, patch_local, obs_patch, cell_offset, frac, obs_value, obs_weight, latent, w_hidden):
    n_patch = latent.shape[0]
    return pl.pallas_call(
        send_kernel,
        out_shape=(
            jax.ShapeDtypeStruct((128, 8, 128), F32),
            jax.ShapeDtypeStruct((8, 256), jnp.int32),
            jax.ShapeDtypeStruct((n_patch, 512, 128), BF16),
        ),
        in_specs=[VMEM] * 7 + [HBM, VMEM],
        out_specs=(HBM, VMEM, HBM),
        scratch_shapes=[
            pltpu.VMEM(latent.shape, BF16),
            pltpu.VMEM((latent.shape[0], 512, 128), BF16),
            pltpu.VMEM((128, 9, 128), F32),
            pltpu.VMEM((128, 9, 128), F32),
            pltpu.VMEM((256, 256), BF16),
            pltpu.SemaphoreType.DMA,
            pltpu.SemaphoreType.DMA,
            pltpu.SemaphoreType.DMA,
            pltpu.SemaphoreType.DMA,
            pltpu.SemaphoreType.DMA,
        ],
        compiler_params=pltpu.CompilerParams(
            vmem_limit_bytes=60 * 1024 * 1024, collective_id=0, has_side_effects=True
        ),
    )(patch_owner, patch_local, obs_patch, cell_offset, frac, obs_value, obs_weight, latent, w_hidden)


def compute(meta, left, recv, w_hidden, b_hidden, w_out):
    n_patch = left.shape[0]
    return pl.pallas_call(
        compute_kernel,
        out_shape=(
            jax.ShapeDtypeStruct((n_patch, 64, 512), F32),
            jax.ShapeDtypeStruct((256, 128), F32),
        ),
        in_specs=[SMEM, HBM, HBM] + [VMEM] * 3,
        out_specs=(HBM, VMEM),
        scratch_shapes=[
            pltpu.VMEM(left.shape, BF16),
            pltpu.VMEM(recv.shape, F32),
            pltpu.VMEM((n_patch, 256, 128), F32),
            pltpu.VMEM((256, 256), BF16),
            pltpu.VMEM((512, 128), BF16),
            pltpu.VMEM((256, 128), F32),
            pltpu.VMEM((2 * TILES, 4, 128), F32),
            pltpu.VMEM((2 * TILES + 8, 128), F32),
            pltpu.VMEM((n_patch, 64, 512), F32),
            pltpu.SemaphoreType.DMA,
            pltpu.SemaphoreType.DMA,
            pltpu.SemaphoreType.DMA,
        ]
        + [pltpu.VMEM((512, 256), BF16)] * UNROLL
        + [pltpu.VMEM((512, 256), F32)] * UNROLL
        + [pltpu.VMEM((64, 256), F32)] * UNROLL
        + [pltpu.VMEM((128, 256), BF16)] * UNROLL,
        compiler_params=pltpu.CompilerParams(vmem_limit_bytes=60 * 1024 * 1024),
    )(meta, left, recv, w_hidden, b_hidden.reshape(1, 256), w_out)


def unpack(patch_owner, obs_patch, score):
    return pl.pallas_call(
        unpack_kernel,
        out_shape=jax.ShapeDtypeStruct(obs_patch.shape, F32),
        in_specs=[VMEM] * 3,
        out_specs=VMEM,
        scratch_shapes=[
            pltpu.VMEM(score.shape, F32),
            pltpu.SemaphoreType.DMA,
            pltpu.SemaphoreType.DMA,
        ],
        compiler_params=pltpu.CompilerParams(
            vmem_limit_bytes=60 * 1024 * 1024, collective_id=1, has_side_effects=True
        ),
    )(patch_owner, obs_patch, score)


def per_device(
    latent,
    patch_owner,
    patch_local,
    obs_patch,
    cell_offset,
    frac,
    obs_value,
    obs_weight,
    w_hidden,
    b_hidden,
    w_out,
):
    recv, meta, left = send(
        patch_owner.T, patch_local.T, obs_patch, cell_offset, frac, obs_value, obs_weight, latent, w_hidden
    )
    grad, score = compute(meta, left, recv, w_hidden, b_hidden, w_out)
    return (grad, unpack(patch_owner.T, obs_patch, score.reshape(128, 2, 128)))


def solution(mesh):
    rows2 = P(AXES, None)
    rows3 = P(AXES, None, None)
    return jax.shard_map(
        per_device,
        mesh=mesh,
        in_specs=(rows3, rows2, rows2, rows2, rows2, rows3, rows2, rows2, P(), P(), P()),
        out_specs=(rows3, rows2),
        check_vma=False,
    )
```

```python
import jax
import jax.numpy as jnp
from jax import lax
from jax.experimental import pallas as pl
from jax.experimental.pallas import tpu as pltpu
from jax.sharding import PartitionSpec as P

root_coef = 0.7978845608028654
cubic_coef = 0.044715
smooth_sq = 0.01
loss_scale = 64.0

alpha = (1.0 / (root_coef * cubic_coef)) ** (1.0 / 3.0)
beta = root_coef * alpha

AXES = ("lat", "lon")
F32, BF16 = jnp.float32, jnp.bfloat16
VMEM = pl.BlockSpec(memory_space=pltpu.VMEM)
SMEM = pl.BlockSpec(memory_space=pltpu.SMEM)
HBM = pl.BlockSpec(memory_space=pl.ANY)
UNROLL = 2
TILES = 168


def three_parts(x):
    high = x.astype(BF16)
    rest = x - high.astype(F32)
    mid = rest.astype(BF16)
    return (high, mid, (rest - mid.astype(F32)).astype(BF16))


def pick(sel, x, dims):
    return sum(
        lax.dot_general(sel, part, (dims, ((), ())), preferred_element_type=F32)
        for part in three_parts(x)
    )


def columns(rows):
    n = rows.shape[1]
    eye = lax.broadcasted_iota(jnp.int32, (n, n), 0) == lax.broadcasted_iota(jnp.int32, (n, n), 1)
    eye = jnp.where(eye, 1.0, 0.0).astype(BF16)
    rows = jnp.concatenate([rows.astype(F32)] * 4, axis=0).astype(BF16)
    dims = (((1,), (1,)), ((), ()))
    return lax.dot_general(eye, rows, dims, preferred_element_type=F32).astype(jnp.int32)


def selectors(owner):
    n = owner.shape[0]
    devices = lax.broadcasted_iota(jnp.int32, (n, 128), 1)
    hit = [(owner[:, e : e + 1] == devices) for e in range(2)]
    both = jnp.where(hit[0] | hit[1], 1.0, 0.0).astype(BF16)
    before = lax.broadcasted_iota(jnp.int32, (n, n), 0) > lax.broadcasted_iota(
        jnp.int32, (n, n), 1
    )
    before = jnp.where(before, 1.0, 0.0).astype(BF16)
    rank = jnp.dot(before, both, preferred_element_type=F32)
    return [
        [jnp.where(hit[e] & (rank == k), 1.0, 0.0) for e in range(2)] for k in range(2)
    ]


def ones_before(entry):
    first = lax.broadcasted_iota(jnp.int32, (128, 128), 0)
    second = lax.broadcasted_iota(jnp.int32, (128, 128), 1)
    tri = jnp.where(first < second, 1.0, 0.0).astype(BF16)
    mine = jnp.where(entry == 1, 1.0, 0.0).astype(BF16)
    return jnp.dot(mine, tri, preferred_element_type=F32).astype(jnp.int32)


def pack(owner, local, entry, offset, frac, value, weight, out):
    sel = selectors(columns(owner[...]))
    off = offset[...]
    row = lax.shift_right_logical(off * 37, 8)
    col = off - row * 7
    fields = [frac[:, 0, :] + row.astype(F32), frac[:, 1, :] + col.astype(F32)]
    fields += [value[...], weight[...]]
    where = entry[...]
    lane = lax.broadcasted_iota(jnp.int32, where.shape, 1)
    one = ones_before(where)
    loc = columns(local[...]).astype(F32) + 1.0
    data, names = [], []
    for e in range(2):
        gap = one if e == 0 else lane - one
        word = jnp.where(where == e, (1 << 20) + gap * 256 + lane, 0)
        for k in range(7):
            come = pltpu.roll(word, 128 - (1 << k), 1)
            stay = jnp.where((word & (256 << k)) == 0, word, 0)
            word = jnp.where((come & (256 << k)) != 0, come, stay)
        source = word & 127
        used = word >= (1 << 20)
        moved = [jnp.take_along_axis(x, source, axis=1) for x in fields]
        moved[3] = jnp.where(used, moved[3], 0.0)
        data.append(jnp.concatenate(moved, axis=1))
        count = jnp.sum(jnp.where(used, 1.0, 0.0), axis=1, keepdims=True)
        names.append(jnp.where(lane < 2, loc[:, e : e + 1], count))
    data = jnp.concatenate(data, axis=0)
    names = jnp.concatenate(names, axis=0).astype(BF16)
    got = []
    for k in range(2):
        two = jnp.concatenate(sel[k], axis=0).astype(BF16)
        rows = pick(two, data, ((0,), (0,)))
        for f in range(4):
            out[:, 4 * k + f, :] = rows[:, f * 128 : (f + 1) * 128]
        got.append(
            lax.dot_general(two, names, (((0,), (0,)), ((), ())), preferred_element_type=F32)
        )
    lane = lax.broadcasted_iota(jnp.int32, (128, 128), 1)
    out[:, 8, :] = jnp.where((lane & 1) == 0, got[0], got[1])


def tiling(named, n_patch):
    flat = named.T
    name_c = jnp.concatenate([named[:, k : k + 1] for k in range(2)], axis=0)
    name_r = jnp.concatenate([flat[k : k + 1] for k in range(2)], axis=1)
    size_r = jnp.concatenate([flat[2 + k : 3 + k] for k in range(2)], axis=1)
    size_b = jnp.broadcast_to(size_r, (16, 256)).astype(BF16)

    def flag(x):
        return jnp.where(x, 1.0, 0.0).astype(BF16)

    def iota(shape, axis):
        return lax.broadcasted_iota(jnp.int32, shape, axis)

    earlier = flag((name_c == name_r) & (iota((256, 256), 0) < iota((256, 256), 1)))
    inside = jnp.dot(size_b, earlier, preferred_element_type=F32)[0:1]
    of_patch = flag(name_c == (iota((256, 128), 1) + 1).astype(F32))
    amount = jnp.dot(size_b, of_patch, preferred_element_type=F32).astype(jnp.int32)
    tiles = lax.shift_right_logical(amount + 255, 8).astype(F32)
    below = flag(iota((128, 128), 0) < iota((128, 128), 1))
    first = jnp.dot(tiles.astype(BF16), below, preferred_element_type=F32)
    spread = flag((iota((128, 256), 0) + 1).astype(F32) == name_r)
    start = jnp.dot(first.astype(BF16), spread, preferred_element_type=F32)[0:1]
    ends = jnp.broadcast_to((first + tiles)[0:1], (128, 128)).T
    ends = jnp.concatenate([ends, ends], axis=1)
    owner = jnp.sum(
        jnp.where(ends <= iota((128, 256), 1).astype(F32), 1.0, 0.0), axis=0, keepdims=True
    )
    owner = jnp.minimum(owner, n_patch - 1.0)
    whole = jnp.broadcast_to(jnp.sum(tiles[0:1], axis=1, keepdims=True), (1, 256))
    rows = [start * 256.0 + inside, size_r, owner, whole]
    return jnp.concatenate(rows + rows, axis=0).astype(jnp.int32)


def send_kernel(
    owner,
    local,
    entry,
    offset,
    frac,
    value,
    weight,
    latent_hbm,
    w_hidden,
    recv_hbm,
    meta,
    left_hbm,
    latent,
    left,
    recv,
    sent,
    w_t,
    send_sem,
    recv_sem,
    latent_sem,
    left_sem,
    out_sem,
):
    fetch = pltpu.make_async_copy(latent_hbm, latent, latent_sem)
    fetch.start()
    lat_size, lon_size = lax.axis_size("lat"), lax.axis_size("lon")
    n_dev = lat_size * lon_size
    me = lax.axis_index("lat") * lon_size + lax.axis_index("lon")
    mesh_id = pl.DeviceIdType.MESH

    def place(i):
        j = lax.rem(me + i, n_dev)
        return j, (lax.div(j, lon_size), lax.rem(j, lon_size))

    barrier = pltpu.get_barrier_semaphore()

    def greet(i, c):
        pl.semaphore_signal(barrier, inc=1, device_id=place(i)[1], device_id_type=mesh_id)
        return c

    lax.fori_loop(1, n_dev, greet, 0, unroll=4)
    pack(owner, local, entry, offset, frac, value, weight, sent)
    pl.semaphore_wait(barrier, n_dev - 1)

    def send(i, c):
        j, there = place(i)
        pltpu.make_async_remote_copy(
            src_ref=sent.at[j],
            dst_ref=recv.at[me],
            send_sem=send_sem,
            recv_sem=recv_sem,
            device_id=there,
            device_id_type=mesh_id,
        ).start()
        return c

    lax.fori_loop(1, n_dev, send, 0, unroll=4)
    recv[me] = sent[me]

    w_t[...] = w_hidden[...].astype(F32).T.astype(BF16)
    lane = lax.broadcasted_iota(jnp.int32, (256, 128), 1)

    def leave(p):
        return pltpu.make_async_copy(left.at[p], left_hbm.at[p], left_sem)

    fetch.wait()

    def project(i, c):
        for j in range(4):
            p = 4 * i + j
            for m in range(2):
                rows = latent[p, :, m * 256 : (m + 1) * 256]
                full = lax.dot_general(
                    w_t[...],
                    jnp.concatenate([rows, rows], axis=0),
                    (((1,), (1,)), ((), ())),
                    preferred_element_type=F32,
                ) * (1.0 / alpha)
                high = full.astype(BF16)
                low = (full - high.astype(F32)).astype(BF16)
                left[p, m * 256 : (m + 1) * 256, :] = jnp.where(lane < 64, high, low)
            leave(p).start()
        return c

    n_patch = latent.shape[0]
    lax.fori_loop(0, n_patch // 4, project, 0)
    pltpu.make_async_remote_copy(
        src_ref=sent.at[pl.ds(0, n_dev - 1)],
        dst_ref=recv.at[pl.ds(0, n_dev - 1)],
        send_sem=send_sem,
        recv_sem=recv_sem,
        device_id=place(1)[1],
        device_id_type=mesh_id,
    ).wait()
    leave_recv = pltpu.make_async_copy(recv.at[:, pl.ds(0, 8), :], recv_hbm, out_sem)
    leave_recv.start()
    meta[...] = tiling(recv[:, 8, :], n_patch)
    leave_recv.wait()
    pltpu.make_async_copy(left, left_hbm, left_sem).wait()


def compute_kernel(
    meta,
    left_hbm,
    recv_hbm,
    w_hidden,
    b_hidden,
    w_out,
    grad,
    score,
    left,
    recv,
    total,
    w_t,
    bias,
    head,
    comp,
    dense,
    ready,
    left_sem,
    recv_sem,
    grad_sem,
    *bufs,
):
    n_patch = left.shape[0]
    n_dev = recv.shape[0]
    derivs, pres, spreads, backs = (bufs[i * UNROLL : (i + 1) * UNROLL] for i in range(4))
    lane = lax.broadcasted_iota(jnp.int32, (256, 128), 1)
    lane4 = lax.broadcasted_iota(jnp.int32, (4, 128), 1)
    lane1 = lax.broadcasted_iota(jnp.int32, (1, 128), 1)

    arrive = pltpu.make_async_copy(recv_hbm, recv, recv_sem)
    arrive.start()
    fetch = pltpu.make_async_copy(left_hbm, left, left_sem)
    fetch.start()
    n_tile = meta[3, 0]

    def tile_of(i):
        return meta[2, i]

    comp[...] = jnp.zeros(comp.shape, F32)
    dense[...] = jnp.zeros(dense.shape, F32)

    def append(i, c):
        for j in range(8):
            s = 8 * i + j
            rows = recv[s]
            for k in range(2):
                base, n = meta[0, 128 * k + s], meta[1, 128 * k + s]
                half, shift = lax.shift_right_logical(base, 7), base & 127
                turned = pltpu.roll(rows[4 * k : 4 * k + 4], shift, 1)
                end = shift + n
                pltpu.store(comp.at[half], turned, mask=(lane4 >= shift) & (lane4 < end))
                pltpu.store(comp.at[half + 1], turned, mask=lane4 < end - 128)
        return c

    w_t[...] = w_hidden[...].astype(F32).T.astype(BF16)
    b_parts = three_parts(jnp.broadcast_to(b_hidden[...] * (1.0 / alpha), (128, 256)).T)
    column = jnp.where(
        lane == 0,
        b_parts[0],
        jnp.where(
            lane == 1, b_parts[1], jnp.where(lane == 2, b_parts[2], jnp.zeros_like(b_parts[0]))
        ),
    )
    bias[0:256, :] = column
    bias[256:512, :] = column
    head[...] = jnp.broadcast_to(w_out[...].astype(F32).reshape(1, 256), (128, 256)).T

    def clear(p, c):
        total[p] = jnp.zeros(total.shape[1:], F32)
        return c

    lax.fori_loop(0, n_patch, clear, 0)
    arrive.wait()
    lax.fori_loop(0, n_dev // 8, append, 0)
    fetch.wait()

    cells = lax.broadcasted_iota(jnp.int32, (8, 256), 0).astype(F32)
    ones = jnp.ones((128, 256), BF16)

    def hidden(i, pre, spread):
        obs = jnp.concatenate([comp[2 * i], comp[2 * i + 1]], axis=1)
        lat = jnp.maximum(1.0 - jnp.abs(obs[0:1] - cells), 0.0)
        lon = jnp.maximum(1.0 - jnp.abs(obs[1:2] - cells), 0.0)
        corner = jnp.concatenate([lat[r : r + 1] * lon for r in range(8)], axis=0)
        spread[...] = corner
        corner_b = corner.astype(BF16)
        right = jnp.concatenate([corner_b, corner_b, ones], axis=0)
        lhs = jnp.concatenate([left[tile_of(i)], bias[...]], axis=1)
        pre[...] = jnp.dot(lhs, right, preferred_element_type=F32)

    def gelu(i, pre, deriv):
        pred = []
        for m in range(2):
            acc = jnp.zeros((8, 256), F32)
            for q in range(4):
                at = m * 256 + q * 64
                v = pre[at : at + 64, :]
                v2 = v * v
                u = jnp.tanh(v * (v2 + beta))
                h = 1.0 + u
                v_b, w_b, h_b = v.astype(BF16), (1.0 - u).astype(BF16), h.astype(BF16)
                slope = v_b * (v_b * v_b + BF16(beta / 3.0))
                deriv[at : at + 64, :] = h_b * (BF16(1.0 / 3.0) + w_b * slope)
                wo = head[q * 64 : q * 64 + 64, :]
                act = v * h * jnp.concatenate([wo, wo], axis=1)
                acc = acc + jnp.sum(act.reshape(8, 8, 256), axis=0)
            pred.append(jnp.sum(acc, axis=0, keepdims=True) * (0.5 * alpha))
        return pred

    def loss(i, pred):
        obs = jnp.concatenate([comp[2 * i], comp[2 * i + 1]], axis=1)
        value = obs[2:3]
        wts = obs[3:4]
        e0, e1, between = pred[0] - value, pred[1] - value, pred[0] - pred[1]
        s0, s1, sm = (x * x + smooth_sq for x in (e0, e1, between))
        r0, r1, rm = (lax.rsqrt(x) for x in (s0, s1, sm))
        pen = wts * (0.5 * (s0 * r0 + s1 * r1) - 0.5 * (sm * rm))
        mid = between * rm
        scaled = (0.5 * loss_scale) * wts
        return scaled * (e0 * r0 - mid), scaled * (e1 * r1 + mid), pen

    def keep(i, pen):
        dense[pl.ds(2 * i + 2, 1), :] = pen[:, :128]
        dense[pl.ds(2 * i + 3, 1), :] = pen[:, 128:]

    def make_back(spread, g, back):
        corner = spread[...]
        back[...] = jnp.concatenate([corner * g[0], corner * g[1]], axis=0).astype(BF16)

    def backward(i, back, deriv):
        both = lax.dot_general(
            deriv[...], back[...], (((1,), (1,)), ((), ())), preferred_element_type=F32
        )
        total[tile_of(jnp.maximum(i, 0))] += jnp.where(lane < 64, both[0:256], both[256:512])

    def some_tiles(i, pen):
        base = i * UNROLL
        for j in range(UNROLL):
            after, prev = (j + 1) % UNROLL, (j + UNROLL - 1) % UNROLL
            hidden(base + j + 1, pres[after], spreads[after])
            pred = gelu(base + j, pres[j], derivs[j])
            keep(base + j - 1, pen)
            backward(base + j - 1, backs[prev], derivs[prev])
            g0, g1, pen = loss(base + j, pred)
            make_back(spreads[j], (g0, g1), backs[j])
        return pen

    hidden(0, pres[0], spreads[0])
    backs[UNROLL - 1][...] = jnp.zeros((128, 256), BF16)
    derivs[UNROLL - 1][...] = jnp.zeros((512, 256), BF16)
    steps = lax.div(n_tile + UNROLL - 1, UNROLL)
    pen = lax.fori_loop(0, steps, some_tiles, jnp.zeros((1, 256), F32))
    keep(steps * UNROLL - 1, pen)
    backward(steps * UNROLL - 1, backs[UNROLL - 1], derivs[UNROLL - 1])

    def give(i, c):
        for j in range(8):
            s = 8 * i + j
            for k in range(2):
                base = meta[0, 128 * k + s]
                half, shift = lax.shift_right_logical(base, 7), base & 127
                row = jnp.where(
                    lane1 >= shift, dense[pl.ds(half + 2, 1), :], dense[pl.ds(half + 3, 1), :]
                )
                score[pl.ds(2 * s + k, 1), :] = pltpu.roll(row, (128 - shift) & 127, 1)
        return c

    lax.fori_loop(0, n_dev // 8, give, 0)

    def leave(p):
        return pltpu.make_async_copy(ready.at[p], grad.at[p], grad_sem)

    def finish(i, c):
        for j in range(16):
            p = 16 * i + j
            both = total[p] * (1.5 * head[...])
            high = both.astype(BF16)
            dims = (((0,), (0,)), ((), ()))
            res = lax.dot_general(high, w_t[...], dims, preferred_element_type=F32)

            ready[p, :, 0:256] = res[0:64]
            ready[p, :, 256:512] = res[64:128]
            leave(p).start()
        return c

    lax.fori_loop(0, n_patch // 16, finish, 0)
    pltpu.make_async_copy(ready, grad, grad_sem).wait()


def unpack_kernel(owner, entry, score, out, back, send_sem, recv_sem):
    lat_size, lon_size = lax.axis_size("lat"), lax.axis_size("lon")
    n_dev = lat_size * lon_size
    me = lax.axis_index("lat") * lon_size + lax.axis_index("lon")
    mesh_id = pl.DeviceIdType.MESH

    def place(i):
        j = lax.rem(me + i, n_dev)
        return j, (lax.div(j, lon_size), lax.rem(j, lon_size))

    barrier = pltpu.get_barrier_semaphore()

    def greet(i, c):
        pl.semaphore_signal(barrier, inc=1, device_id=place(i)[1], device_id_type=mesh_id)
        return c

    lax.fori_loop(1, n_dev, greet, 0, unroll=4)
    sel = selectors(columns(owner[...]))
    where = entry[...]
    lane = lax.broadcasted_iota(jnp.int32, where.shape, 1)
    one = ones_before(where)
    pl.semaphore_wait(barrier, n_dev - 1)

    def send_one(i, c):
        j, there = place(i)
        pltpu.make_async_remote_copy(
            src_ref=score.at[j],
            dst_ref=back.at[me],
            send_sem=send_sem,
            recv_sem=recv_sem,
            device_id=there,
            device_id_type=mesh_id,
        ).start()
        return c

    lax.fori_loop(1, n_dev, send_one, 0, unroll=4)
    back[me] = score[me]
    pltpu.make_async_remote_copy(
        src_ref=score.at[pl.ds(0, n_dev - 1)],
        dst_ref=back.at[pl.ds(0, n_dev - 1)],
        send_sem=send_sem,
        recv_sem=recv_sem,
        device_id=place(1)[1],
        device_id_type=mesh_id,
    ).wait()
    got = []
    for e in range(2):
        rows = sum(pick(sel[k][e].astype(BF16), back[:, k, :], ((1,), (0,))) for k in range(2))
        got.append(jnp.take_along_axis(rows, one if e == 1 else lane - one, axis=1))
    out[...] = jnp.where(where == 0, got[0], got[1])


def send(patch_owner, patch_local, obs_patch, cell_offset, frac, obs_value, obs_weight, latent, w_hidden):
    n_patch = latent.shape[0]
    return pl.pallas_call(
        send_kernel,
        out_shape=(
            jax.ShapeDtypeStruct((128, 8, 128), F32),
            jax.ShapeDtypeStruct((8, 256), jnp.int32),
            jax.ShapeDtypeStruct((n_patch, 512, 128), BF16),
        ),
        in_specs=[VMEM] * 7 + [HBM, VMEM],
        out_specs=(HBM, VMEM, HBM),
        scratch_shapes=[
            pltpu.VMEM(latent.shape, BF16),
            pltpu.VMEM((latent.shape[0], 512, 128), BF16),
            pltpu.VMEM((128, 9, 128), F32),
            pltpu.VMEM((128, 9, 128), F32),
            pltpu.VMEM((256, 256), BF16),
            pltpu.SemaphoreType.DMA,
            pltpu.SemaphoreType.DMA,
            pltpu.SemaphoreType.DMA,
            pltpu.SemaphoreType.DMA,
            pltpu.SemaphoreType.DMA,
        ],
        compiler_params=pltpu.CompilerParams(
            vmem_limit_bytes=60 * 1024 * 1024, collective_id=0, has_side_effects=True
        ),
    )(patch_owner, patch_local, obs_patch, cell_offset, frac, obs_value, obs_weight, latent, w_hidden)


def compute(meta, left, recv, w_hidden, b_hidden, w_out):
    n_patch = left.shape[0]
    return pl.pallas_call(
        compute_kernel,
        out_shape=(
            jax.ShapeDtypeStruct((n_patch, 64, 512), F32),
            jax.ShapeDtypeStruct((256, 128), F32),
        ),
        in_specs=[SMEM, HBM, HBM] + [VMEM] * 3,
        out_specs=(HBM, VMEM),
        scratch_shapes=[
            pltpu.VMEM(left.shape, BF16),
            pltpu.VMEM(recv.shape, F32),
            pltpu.VMEM((n_patch, 256, 128), F32),
            pltpu.VMEM((256, 256), BF16),
            pltpu.VMEM((512, 128), BF16),
            pltpu.VMEM((256, 128), F32),
            pltpu.VMEM((2 * TILES, 4, 128), F32),
            pltpu.VMEM((2 * TILES + 8, 128), F32),
            pltpu.VMEM((n_patch, 64, 512), F32),
            pltpu.SemaphoreType.DMA,
            pltpu.SemaphoreType.DMA,
            pltpu.SemaphoreType.DMA,
        ]
        + [pltpu.VMEM((512, 256), BF16)] * UNROLL
        + [pltpu.VMEM((512, 256), F32)] * UNROLL
        + [pltpu.VMEM((64, 256), F32)] * UNROLL
        + [pltpu.VMEM((128, 256), BF16)] * UNROLL,
        compiler_params=pltpu.CompilerParams(vmem_limit_bytes=60 * 1024 * 1024),
    )(meta, left, recv, w_hidden, b_hidden.reshape(1, 256), w_out)


def unpack(patch_owner, obs_patch, score):
    return pl.pallas_call(
        unpack_kernel,
        out_shape=jax.ShapeDtypeStruct(obs_patch.shape, F32),
        in_specs=[VMEM] * 3,
        out_specs=VMEM,
        scratch_shapes=[
            pltpu.VMEM(score.shape, F32),
            pltpu.SemaphoreType.DMA,
            pltpu.SemaphoreType.DMA,
        ],
        compiler_params=pltpu.CompilerParams(
            vmem_limit_bytes=60 * 1024 * 1024, collective_id=1, has_side_effects=True
        ),
    )(patch_owner, obs_patch, score)


def per_device(
    latent,
    patch_owner,
    patch_local,
    obs_patch,
    cell_offset,
    frac,
    obs_value,
    obs_weight,
    w_hidden,
    b_hidden,
    w_out,
):
    recv, meta, left = send(
        patch_owner.T, patch_local.T, obs_patch, cell_offset, frac, obs_value, obs_weight, latent, w_hidden
    )
    grad, score = compute(meta, left, recv, w_hidden, b_hidden, w_out)
    return (grad, unpack(patch_owner.T, obs_patch, score.reshape(128, 2, 128)))


def solution(mesh):
    rows2 = P(AXES, None)
    rows3 = P(AXES, None, None)
    return jax.shard_map(
        per_device,
        mesh=mesh,
        in_specs=(rows3, rows2, rows2, rows2, rows2, rows3, rows2, rows2, P(), P(), P()),
        out_specs=(rows3, rows2),
        check_vma=False,
    )
```
